32 devices in a mesh: clip: 2 (over x), row: 4 (over y, core), tm: 4 (over z).
Axes of the slice: x: 2, y: 2, z: 4, core: 2. Of those that a mesh axis runs over, the one named last changes fastest.
Arguments:
- frames: bfloat16 [16, 3, 16, 1024], P('clip', None, 'tm', 'row'), may hold values from -6 to 6
- keep_list: int32 [16], P('clip'), may hold values from -1 to 7, as said below
- train_slot: int32 [8], replicated, may hold values from 0 to 7, as said below
- stem_weight: bfloat16 [81, 128], replicated, may hold values from -0.625 to 0.625
- stem_gain: float32 [128], replicated, may hold values from 0.1 to 1.9
- stem_shift: float32 [128], replicated, may hold values from -3 to 3
- mixer_weight: bfloat16 [3, 3, 384, 256], replicated, may hold values from -0.109375 to 0.109375
- mixer_gain: float32 [256], replicated, may hold values from 0.1 to 1.9
- mixer_shift: float32 [256], replicated, may hold values from -3 to 3
- down_weight: bfloat16 [1024, 256], replicated, may hold values from -0.1875 to 0.1875
- down_bias: float32 [256], replicated, may hold values from -3 to 3
Outputs:
- latents: bfloat16 [8, 8, 8, 32, 256], P('clip', 'tm', 'row')
The draws below stay inside these ranges and needn't reach their ends.
Inputs may be any that keep to these rules, and one draw needn't show every extreme that they name: `keep_list`: each encoder position 0 to 7 is named by exactly one slot, and -1 marks a dropped slot; encoder position e belongs to index e // 4 of clip. `train_slot`: A permutation; training position t belongs to index t // 4 of clip; at most 2 encoder positions of one index of clip go to one index of clip.
All inputs are finite; a program needn't handle non-finite values.
Results may differ from the reference program's by a relative error of at most 0.0053.
Values may be sent and summed in bfloat16 or wider, within the bound.
A program may use at most 64 MiB of HBM per device.

```python
import jax
import jax.numpy as jnp
from jax import lax

C_IN = 3
C_MID = 128
C_OUT = 256
GROUPS = 32
SLOTS_DEV = 8
ENC_DEV = 4
COLS = 64
SLOTS = 16
TRAIN = 8
FRAMES = 16
ROWS = 16


def draw_frames(key, part):
    noise_key, offset_key = jax.random.split(key)
    time_pos = jnp.arange(FRAMES, dtype=jnp.float32) / max(FRAMES - 1, 1)
    row_pos = (jnp.arange(ROWS * COLS) // COLS).astype(jnp.float32) / max(ROWS - 1, 1)
    ramp = 0.5 + 0.5 * (time_pos[:, None] + row_pos[None, :])
    shape_full = (SLOTS, C_IN, FRAMES, ROWS * COLS)
    noise = jax.random.normal(noise_key, shape_full, jnp.float32)
    offset = 0.3 * jax.random.normal(offset_key, (SLOTS, C_IN), jnp.float32)
    return jnp.clip(offset[:, :, None, None] + ramp * noise, -6.0, 6.0).astype(jnp.bfloat16)


def draw_keep_list(key, part):
    busy_key, rank_key, place_key = jax.random.split(jax.random.fold_in(key, 11), 3)
    group_count = SLOTS // SLOTS_DEV
    busiest = jax.random.randint(busy_key, (), 0, group_count)
    ranks = jax.random.permutation(rank_key, SLOTS).astype(jnp.int32)
    slot_ids = jnp.arange(SLOTS, dtype=jnp.int32)
    score = jnp.where(slot_ids // SLOTS_DEV == busiest, slot_ids % SLOTS_DEV - SLOTS_DEV, ranks)
    order = jnp.argsort(score, stable=True)
    chosen = order[:TRAIN]
    positions = jax.random.permutation(place_key, TRAIN).astype(jnp.int32)
    return jnp.full((SLOTS,), -1, jnp.int32).at[chosen].set(positions)


def draw_train_slot(key, part):
    keys = jax.random.split(jax.random.fold_in(key, 23), 5)
    group_count = TRAIN // ENC_DEV
    outer = jax.random.permutation(keys[0], group_count).astype(jnp.int32)
    inner = jax.random.permutation(keys[1], group_count).astype(jnp.int32)
    offsets = jax.random.permutation(keys[2], group_count).astype(jnp.int32)
    turn = jax.random.randint(keys[3], (group_count,), 0, ENC_DEV).astype(jnp.int32)
    positions = jnp.arange(TRAIN, dtype=jnp.int32)
    sender = positions // ENC_DEV
    within = (positions % ENC_DEV + turn[sender]) % ENC_DEV
    destination = outer[(inner[sender] + offsets[within % group_count]) % group_count]
    score = jax.random.permutation(keys[4], TRAIN).astype(jnp.int32)
    same = destination[None, :] == destination[:, None]
    lower = score[None, :] < score[:, None]
    landing = jnp.sum((same & lower).astype(jnp.int32), axis=1)
    return (destination * ENC_DEV + landing).astype(jnp.int32)


def gaussian(rng, dims, deviation, bound, kind=jnp.bfloat16):
    drawn = jax.random.normal(rng, dims, jnp.float32) * deviation
    return jnp.minimum(jnp.maximum(drawn, -bound), bound).astype(kind)


def setup_inputs(seed: int = 0) -> dict:
    key_of = jax.random.split(jax.random.key(seed), 12)
    frames = draw_frames(jax.random.fold_in(key_of[11], 71), 0)
    keep_list = draw_keep_list(jax.random.fold_in(key_of[11], 71), 0)
    train_slot = draw_train_slot(jax.random.fold_in(key_of[11], 71), 0)
    stem_weight = gaussian(key_of[3], (27 * C_IN, C_MID), (27 * C_IN) ** -0.5, 0.625)
    stem_gain = jnp.clip(1.0 + 0.18 * jax.random.normal(key_of[4], (C_MID,), jnp.float32), 0.1, 1.9)
    stem_shift = gaussian(key_of[5], (C_MID,), 0.5, 3.0, jnp.float32)
    mixer_weight = gaussian(key_of[6], (3, 3, 3 * C_MID, C_OUT), (27 * C_MID) ** -0.5, 0.109375)
    mixer_gain = jnp.clip(1.0 + 0.18 * jax.random.normal(key_of[7], (C_OUT,), jnp.float32), 0.1, 1.9)
    mixer_shift = gaussian(key_of[8], (C_OUT,), 0.5, 3.0, jnp.float32)
    down_weight = gaussian(key_of[9], (4 * C_OUT, C_OUT), (4 * C_OUT) ** -0.5, 0.1875)
    down_bias = gaussian(key_of[10], (C_OUT,), 0.5, 3.0, jnp.float32)
    return {"frames": frames, "keep_list": keep_list, "train_slot": train_slot, "stem_weight": stem_weight, "stem_gain": stem_gain, "stem_shift": stem_shift, "mixer_weight": mixer_weight, "mixer_gain": mixer_gain, "mixer_shift": mixer_shift, "down_weight": down_weight, "down_bias": down_bias}


eps = 1e-06

def product(left, right):
    return jnp.dot(left.astype(jnp.float32), right.astype(jnp.float32), precision=lax.Precision.HIGHEST)

def norm_silu(hidden, gain, shift):
    cell_n, chan_n = hidden.shape
    per_group = chan_n // GROUPS
    value_sum = lax.optimization_barrier(jnp.sum(hidden, axis=0)).reshape(GROUPS, per_group).sum(-1)
    square_sum = lax.optimization_barrier(jnp.sum(hidden * hidden, axis=0)).reshape(GROUPS, per_group).sum(-1)
    cell_count = cell_n * per_group
    group_mean = value_sum / cell_count
    spread = square_sum / cell_count - group_mean * group_mean
    inverse = lax.rsqrt(spread + eps)
    mean_full = jnp.repeat(group_mean, per_group)[None, :]
    scale_full = jnp.repeat(inverse, per_group)[None, :] * gain
    return jax.nn.silu((hidden - mean_full) * scale_full + shift)

def surround(volume):
    extended = jnp.concatenate([volume[:1], volume[:1], volume], axis=0)
    return jnp.pad(extended, ((0, 0), (1, 1), (1, 1), (0, 0)))

def encode_clip(clip, stem_weight, stem_gain, stem_shift, mixer_weight, mixer_gain, mixer_shift, down_weight, down_bias):
    volume = clip.reshape(C_IN, FRAMES, ROWS, COLS).transpose(1, 2, 3, 0)
    padded = surround(volume)
    tap_views = []
    for time_tap in range(3):
        for row_tap in range(3):
            for col_tap in range(3):
                tap_views.append(padded[time_tap:time_tap + FRAMES, row_tap:row_tap + ROWS, col_tap:col_tap + COLS])
    patches = jnp.concatenate(tap_views, axis=-1).reshape(FRAMES * ROWS * COLS, 27 * C_IN)
    stem = product(patches, stem_weight)
    hidden = norm_silu(stem, stem_gain, stem_shift).astype(jnp.bfloat16)
    padded = surround(hidden.reshape(FRAMES, ROWS, COLS, -1))
    accumulated = jnp.zeros((FRAMES * ROWS * COLS, mixer_weight.shape[3]), jnp.float32)
    for time_tap in range(3):
        for row_tap in range(3):
            tap_strip = jnp.concatenate([padded[time_tap:time_tap + FRAMES, row_tap:row_tap + ROWS, col_tap:col_tap + COLS] for col_tap in range(3)], axis=-1)
            accumulated = accumulated + product(tap_strip.reshape(-1, tap_strip.shape[-1]), mixer_weight[time_tap, row_tap])
    activated = norm_silu(accumulated, mixer_gain, mixer_shift).astype(jnp.bfloat16)
    activated = activated.reshape(FRAMES, ROWS, COLS, -1)
    pooled = ((activated[0::2].astype(jnp.float32) + activated[1::2].astype(jnp.float32)) * 0.5).astype(jnp.bfloat16)
    chan_out = pooled.shape[-1]
    blocks = pooled.reshape(FRAMES // 2, ROWS // 2, 2, COLS // 2, 2, chan_out).transpose(0, 1, 3, 2, 4, 5).reshape(-1, 4 * chan_out)
    latent = product(blocks, down_weight) + down_bias
    return latent.astype(jnp.bfloat16).reshape(FRAMES // 2, ROWS // 2, COLS // 2, chan_out)

def reference(frames, keep_list, train_slot, stem_weight, stem_gain, stem_shift, mixer_weight, mixer_gain, mixer_shift, down_weight, down_bias):
    target = jnp.where(keep_list >= 0, keep_list, TRAIN).astype(jnp.int32)
    slot_of_encoder = jnp.zeros((TRAIN,), jnp.int32).at[target].set(jnp.arange(SLOTS, dtype=jnp.int32), mode='drop')
    encoder_of_train = jnp.zeros((TRAIN,), jnp.int32).at[train_slot].set(jnp.arange(TRAIN, dtype=jnp.int32))
    source = slot_of_encoder[encoder_of_train]

    def encode_one(slot_index):
        clip = lax.dynamic_index_in_dim(frames, slot_index, 0, keepdims=False)
        return encode_clip(clip, stem_weight, stem_gain, stem_shift, mixer_weight, mixer_gain, mixer_shift, down_weight, down_bias)
    return lax.map(encode_one, source)
```

```python
import functools

import jax
import jax.numpy as jnp
from jax import lax
from jax.experimental import pallas as pl
from jax.experimental.pallas import tpu as pltpu
from jax.sharding import PartitionSpec as P

GROUPS = 32
COLS = 64
HALO = 2
TAPS = 3
MESH = pl.DeviceIdType.MESH
F32 = jnp.float32
BF16 = jnp.bfloat16

eps = 1e-06


def iota(shape, dim):
    return lax.broadcasted_iota(jnp.int32, shape, dim)


def quot(value, by):
    return lax.shift_right_logical(value * (65536 // by + 1), 16)


def rest(value, by):
    return value - quot(value, by) * by


def dot(left, right):
    return jnp.dot(left, right, preferred_element_type=F32)


def silu(value):
    half = value * 0.5
    return half + half * jnp.tanh(half)


def one_hot(flag):
    return jnp.where(flag, 1.0, 0.0).astype(BF16)


def kernel(
    sizes,
    frames_ref,
    keep_ref,
    train_ref,
    stem_w_ref,
    stem_gain_ref,
    stem_shift_ref,
    mixer_gain_ref,
    mixer_shift_ref,
    down_bias_ref,
    mixer_hbm,
    down_hbm,
    out_ref,
    packed,
    landed,
    stem_scr,
    hidden_scr,
    mixer_scr,
    mixer_w,
    down_w,
    sums1,
    sums2,
    load_sem,
    frame_send,
    frame_recv,
    sum_send,
    sum_recv,
):
    clip_n, row_dev, time_dev, clips, chan, frame_n, row_n, rounds = sizes
    cells = row_n * COLS
    c = lax.axis_index("clip")
    r = lax.axis_index("row")
    t = lax.axis_index("tm")
    me = r * time_dev + t
    peers = row_dev * time_dev
    per_clip = frame_n * chan
    halo_cells = HALO * COLS
    wide = cells + 2 * halo_cells
    out_cells = cells + 2 * COLS
    ext_f = frame_n + HALO
    chan_mid = stem_w_ref.shape[1]
    chan_out = mixer_w.shape[1]

    load_mixer = pltpu.make_async_copy(mixer_hbm, mixer_w, load_sem.at[0])
    load_down = pltpu.make_async_copy(down_hbm, down_w, load_sem.at[1])
    load_mixer.start()
    load_down.start()

    landed[...] = jnp.zeros_like(landed)

    barrier = pltpu.get_barrier_semaphore()
    for j in range(1, peers):
        other = lax.rem(me + j, peers)
        pl.semaphore_signal(
            barrier,
            inc=1,
            device_id={"row": other // time_dev, "tm": lax.rem(other, time_dev)},
            device_id_type=MESH,
        )
    rows_near = 1 + (r > 0).astype(jnp.int32) + (r < row_dev - 1).astype(jnp.int32)
    times_near = 1 + (t > 0).astype(jnp.int32) + (t < time_dev - 1).astype(jnp.int32)
    for k in range(1, clip_n):
        for dr in (-1, 0, 1):
            for dt in (-1, 0, 1):

                @pl.when((r + dr >= 0) & (r + dr < row_dev) & (t + dt >= 0) & (t + dt < time_dev))
                def _():
                    pl.semaphore_signal(
                        barrier,
                        inc=1,
                        device_id={"clip": lax.rem(c + k, clip_n), "row": r + dr, "tm": t + dt},
                        device_id_type=MESH,
                    )

    slot_n = keep_ref.shape[1]
    enc_n = train_ref.shape[1]
    rows_in = slot_n * per_clip
    rows_out = enc_n * per_clip
    named = one_hot(iota((enc_n, slot_n), 0) == keep_ref[...])
    spread = one_hot(quot(iota((slot_n, rows_in), 1), per_clip) == iota((slot_n, rows_in), 0))
    by_row = dot(named, spread).astype(BF16)
    wanted = one_hot(quot(iota((rows_out, enc_n), 0), per_clip) == train_ref[...])
    chosen = dot(wanted, by_row)
    row_at = rest(iota((rows_out, rows_in), 0), per_clip)
    col_at = rest(iota((rows_out, rows_in), 1), per_clip)
    same = (quot(row_at, chan) == rest(col_at, frame_n)) & (
        rest(row_at, chan) == quot(col_at, frame_n)
    )
    chosen = jnp.where(same, chosen, 0.0).astype(BF16)
    picked = dot(chosen, frames_ref[...]).astype(BF16)
    packed[...] = picked.reshape(packed.shape)

    pl.semaphore_wait(barrier, peers - 1 + (clip_n - 1) * rows_near * times_near)

    def frame_copy(k, dt, dr):
        if dr == 0:
            src, dst = pl.ds(0, cells), pl.ds(halo_cells, cells)
        elif dr == 1:
            src, dst = pl.ds(cells - halo_cells, halo_cells), pl.ds(0, halo_cells)
        else:
            src, dst = pl.ds(0, halo_cells), pl.ds(halo_cells + cells, halo_cells)
        goal = lax.rem(c + k, clip_n)
        return pltpu.make_async_remote_copy(
            src_ref=packed.at[goal, :, src],
            dst_ref=landed.at[k, dt, :, dst],
            send_sem=frame_send.at[k, dt, dr + 1],
            recv_sem=frame_recv.at[k, dt, dr + 1],
            device_id={"clip": goal, "row": r + dr, "tm": t + dt},
            device_id_type=MESH,
        )

    moves = [
        (k, dt, dr)
        for k in range(clip_n - 1, -1, -1)
        for dt in (1, 0)
        for dr in (1, -1, 0)
        if (k, dt, dr) != (0, 0, 0)
    ]

    def each_move(sign, act):
        for k, dt, dr in moves:
            rr, tt = r + sign * dr, t + sign * dt
            if dr == 0 and dt == 0:
                act(frame_copy(k, dt, dr))
                continue

            @pl.when((rr >= 0) & (rr < row_dev) & (tt >= 0) & (tt < time_dev))
            def _():
                act(frame_copy(k, dt, dr))

    each_move(1, lambda copy: copy.start())
    landed[0, 0, :, halo_cells : halo_cells + cells] = packed[c]

    frames_wide = 2 * frame_n
    lines = frames_wide * chan
    depth = 256
    stem_w = stem_w_ref[...]
    taps_n = stem_w.shape[0]
    at = iota((depth, taps_n), 0)
    shift_at = quot(at, lines)
    in_shift = rest(at, lines)
    frame_at = quot(in_shift, chan)
    chan_at = in_shift - frame_at * chan
    tap_at = iota((depth, taps_n), 1)
    columns = []
    for f in range(ext_f):
        a = frame_at - f
        index = (a * (TAPS * TAPS) + shift_at) * chan + chan_at
        ok = (a >= 0) & (a < TAPS) & (at < TAPS * TAPS * lines) & (index == tap_at)
        columns.append(dot(one_hot(ok), stem_w).astype(BF16))
    stem_big = jnp.concatenate(columns, axis=1)

    lane = iota((128, 128), 1)
    source = iota((128, 128), 0)
    in_row = lane & (COLS - 1)
    col = 2 * (in_row & (COLS // 2 - 1)) + jnp.where(in_row >= COLS // 2, 1, 0)
    tables = []
    for tap in range(TAPS):
        moved = col + (tap - 1)
        ok = (moved >= 0) & (moved < COLS) & (source == (lane - in_row) + moved)
        tables.append(one_hot(ok))
    col_table = jnp.concatenate(tables, axis=1)

    half_rows = clips * per_clip
    total_rows = 2 * half_rows
    row_at = iota((total_rows, total_rows), 0)
    clip_at = quot(row_at, lines)
    in_clip = rest(row_at, lines)
    frame_at = quot(in_clip, chan)
    chan_at = in_clip - frame_at * chan
    base = clip_at * per_clip + chan_at
    before = jnp.where(t > 0, half_rows + base + frame_at * chan, base)
    goal = jnp.where(frame_at >= frame_n, base + (frame_at - frame_n) * chan, before)
    order = one_hot(goal == iota((total_rows, total_rows), 1))

    each_move(-1, lambda copy: copy.wait_recv())

    volume = landed[0].astype(F32)
    for k in range(1, clip_n):
        volume = volume + landed[k].astype(F32)
    volume = volume.astype(BF16).reshape(total_rows, wide)
    volume = dot(order, volume).astype(BF16)
    blocks = wide // 128
    stacked = jnp.concatenate(
        [volume[:, b * 128 : (b + 1) * 128] for b in range(blocks)], axis=0
    )
    shifted = dot(stacked, col_table)
    views = []
    by_tap = []
    for tap in range(TAPS):
        by_tap.append(
            jnp.concatenate(
                [
                    shifted[b * total_rows : (b + 1) * total_rows, tap * 128 : (tap + 1) * 128]
                    for b in range(blocks)
                ],
                axis=1,
            )
        )
    for row_tap in range(TAPS):
        for tap in range(TAPS):
            if row_tap % 2:
                views.append(
                    pltpu.roll(by_tap[tap], wide - row_tap * COLS, 1)[:, :out_cells]
                )
            else:
                views.append(by_tap[tap][:, row_tap * COLS : row_tap * COLS + out_cells])
    filler = jnp.zeros((depth - TAPS * TAPS * lines, out_cells), F32)

    def sum_copy(buffer, number, index, j):
        other = lax.rem(me + j, peers)
        return pltpu.make_async_remote_copy(
            src_ref=buffer.at[index, me],
            dst_ref=buffer.at[index, me],
            send_sem=sum_send.at[number, j],
            recv_sem=sum_recv.at[number, j],
            device_id={"row": other // time_dev, "tm": lax.rem(other, time_dev)},
            device_id_type=MESH,
        )

    def send_sums(buffer, number, index):
        for j in range(1, peers):
            sum_copy(buffer, number, index, j).start()

    def take_sums(buffer, number, index, gain, shift):
        for j in range(1, peers):
            sum_copy(buffer, number, index, j).wait_recv()
        total = buffer[index, 0]
        for j in range(1, peers):
            total = total + buffer[index, j]
        chan_n = total.shape[1]
        per_group = chan_n // GROUPS
        joined = jnp.where(
            quot(iota((chan_n, chan_n), 0), per_group) == quot(iota((chan_n, chan_n), 1), per_group),
            1.0,
            0.0,
        )
        total = jnp.dot(
            total, joined, preferred_element_type=F32, precision=lax.Precision.HIGHEST
        )
        count = peers * frame_n * cells * per_group
        total = total * (1.0 / count)
        half = total.shape[0] // 2
        mean = total[:half]
        inverse = lax.rsqrt(total[half:] - mean * mean + eps)
        scale = inverse * gain
        return scale, shift - mean * scale

    per_round = clips // rounds
    for turn in range(rounds):
        for pos in range(per_round):
            k = turn * per_round + pos
            patches = jnp.concatenate(
                [view[k * lines : (k + 1) * lines] for view in views] + [filler], axis=0
            ).astype(BF16)
            stem = lax.dot_general(
                patches, stem_big, (((0,), (0,)), ((), ())), preferred_element_type=F32
            )
            stem_scr[k] = stem
            own = stem[COLS : COLS + cells, HALO * chan_mid :]
            values = jnp.sum(own, axis=0, keepdims=True)
            squares = jnp.sum(own * own, axis=0, keepdims=True)
            value_sum = values[:, :chan_mid]
            square_sum = squares[:, :chan_mid]
            for f in range(1, frame_n):
                value_sum = value_sum + values[:, f * chan_mid : (f + 1) * chan_mid]
                square_sum = square_sum + squares[:, f * chan_mid : (f + 1) * chan_mid]
            sums1[turn, me, pos : pos + 1, :] = value_sum
            sums1[turn, me, per_round + pos : per_round + pos + 1, :] = square_sum
        send_sums(sums1, turn, turn)

    top = jnp.where(r > 0, 1.0, 0.0).astype(F32)
    bottom = jnp.where(r < row_dev - 1, 1.0, 0.0).astype(F32)
    ext_rows = row_n + 2
    half_cols = COLS // 2
    x_at = iota((ext_rows * half_cols, chan_mid), 0) & (half_cols - 1)

    def norm_first(k, scale, shift):
        for f in range(ext_f):
            value = stem_scr[k, :, f * chan_mid : (f + 1) * chan_mid]
            value = silu(value * scale + shift)
            value = jnp.concatenate(
                [
                    value[:COLS] * top,
                    value[COLS : COLS + cells],
                    value[COLS + cells :] * bottom,
                ],
                axis=0,
            )
            parts = value.reshape(ext_rows, 2, half_cols, chan_mid)
            even, odd = parts[:, 0], parts[:, 1]
            flat = (ext_rows * half_cols, chan_mid)
            left = jnp.where(x_at == 0, 0.0, pltpu.roll(odd.reshape(flat), 1, 0))
            right = jnp.where(
                x_at == half_cols - 1, 0.0, pltpu.roll(even.reshape(flat), flat[0] - 1, 0)
            )
            left = left.reshape(even.shape)
            right = right.reshape(even.shape)
            before = jnp.stack([left, even], axis=1).reshape(value.shape)
            after = jnp.stack([odd, right], axis=1).reshape(value.shape)
            hidden_scr[k, f, :, :chan_mid] = before.astype(BF16)
            hidden_scr[k, f, :, chan_mid : 2 * chan_mid] = value.astype(BF16)
            hidden_scr[k, f, :, 2 * chan_mid :] = after.astype(BF16)

    def mix(k, turn, pos):
        value_sum = jnp.zeros((1, chan_out), F32)
        square_sum = jnp.zeros((1, chan_out), F32)
        for f in range(frame_n):
            strip = jnp.concatenate(
                [
                    hidden_scr[k, f + a, b * COLS : b * COLS + cells, :]
                    for a in range(TAPS)
                    for b in range(TAPS)
                ],
                axis=1,
            )
            mixed = dot(strip, mixer_w[...])
            mixer_scr[k, f] = mixed
            value_sum = value_sum + jnp.sum(mixed, axis=0, keepdims=True)
            square_sum = square_sum + jnp.sum(mixed * mixed, axis=0, keepdims=True)
        sums2[turn, me, pos : pos + 1, :] = value_sum
        sums2[turn, me, per_round + pos : per_round + pos + 1, :] = square_sum

    load_mixer.wait()
    for turn in range(rounds):
        scale, shift = take_sums(sums1, turn, turn, stem_gain_ref[...], stem_shift_ref[...])
        for pos in range(per_round):
            k = turn * per_round + pos
            norm_first(k, scale[pos : pos + 1], shift[pos : pos + 1])
            mix(k, turn, pos)
        send_sums(sums2, rounds + turn, turn)

    load_down.wait()
    bias = down_bias_ref[...]
    pairs = frame_n // 2
    out_rows = row_n // 2
    for turn in range(rounds):
        scale, shift = take_sums(
            sums2, rounds + turn, turn, mixer_gain_ref[...], mixer_shift_ref[...]
        )
        for pos in range(per_round):
            k = turn * per_round + pos
            squares = []
            for pair in range(pairs):
                acts = []
                for f in (2 * pair, 2 * pair + 1):
                    value = mixer_scr[k, f] * scale[pos : pos + 1] + shift[pos : pos + 1]
                    acts.append(silu(value).astype(BF16).astype(F32))
                pooled = ((acts[0] + acts[1]) * 0.5).astype(BF16)
                pooled = pooled.reshape(out_rows, 2, 2, half_cols, chan_out)
                squares.append(
                    jnp.concatenate(
                        [
                            pooled[:, p, q].reshape(out_rows * half_cols, chan_out)
                            for p in range(2)
                            for q in range(2)
                        ],
                        axis=1,
                    )
                )
            block = jnp.concatenate(squares, axis=0)
            latent = dot(block, down_w[...]) + bias
            size = block.shape[0]
            out_ref[k * size : (k + 1) * size, :] = latent.astype(BF16)

    each_move(1, lambda copy: copy.wait_send())
    for turn in range(rounds):
        for j in range(1, peers):
            sum_copy(sums1, turn, turn, j).wait_send()
            sum_copy(sums2, rounds + turn, turn, j).wait_send()


def local(
    frames,
    keep_list,
    train_slot,
    stem_weight,
    stem_gain,
    stem_shift,
    mixer_weight,
    mixer_gain,
    mixer_shift,
    down_weight,
    down_bias,
):
    clip_n = lax.axis_size("clip")
    row_dev = lax.axis_size("row")
    time_dev = lax.axis_size("tm")
    slots, chan, frame_n, cells = frames.shape
    clips = train_slot.shape[0] // clip_n
    row_n = cells // COLS
    chan_mid = stem_weight.shape[1]
    chan_out = mixer_weight.shape[3]
    rounds = 2 if clips % 2 == 0 else 1
    per_round = clips // rounds
    peers = row_dev * time_dev
    ext_f = frame_n + HALO
    out_cells = cells + 2 * COLS
    sizes = (clip_n, row_dev, time_dev, clips, chan, frame_n, row_n, rounds)
    out_rows = clips * (frame_n // 2) * (row_n // 2) * (COLS // 2)
    mixer_flat = mixer_weight.reshape(-1, chan_out)
    vmem = pl.BlockSpec(memory_space=pltpu.VMEM)
    hbm = pl.BlockSpec(memory_space=pl.ANY)
    out = pl.pallas_call(
        functools.partial(kernel, sizes),
        out_shape=jax.ShapeDtypeStruct((out_rows, chan_out), BF16),
        in_specs=[vmem] * 9 + [hbm] * 2,
        out_specs=vmem,
        scratch_shapes=[
            pltpu.VMEM((clip_n, clips * frame_n * chan, cells), BF16),
            pltpu.VMEM((clip_n, 2, clips * frame_n * chan, cells + 2 * HALO * COLS), BF16),
            pltpu.VMEM((clips, out_cells, ext_f * chan_mid), F32),
            pltpu.VMEM((clips, ext_f, out_cells, TAPS * chan_mid), BF16),
            pltpu.VMEM((clips, frame_n, cells, chan_out), F32),
            pltpu.VMEM(mixer_flat.shape, BF16),
            pltpu.VMEM(down_weight.shape, BF16),
            pltpu.VMEM((rounds, peers, 2 * per_round, chan_mid), F32),
            pltpu.VMEM((rounds, peers, 2 * per_round, chan_out), F32),
            pltpu.SemaphoreType.DMA((2,)),
            pltpu.SemaphoreType.DMA((clip_n, 2, 3)),
            pltpu.SemaphoreType.DMA((clip_n, 2, 3)),
            pltpu.SemaphoreType.DMA((2 * rounds, peers)),
            pltpu.SemaphoreType.DMA((2 * rounds, peers)),
        ],
        compiler_params=pltpu.CompilerParams(
            collective_id=0, has_side_effects=True, vmem_limit_bytes=50 * 1024 * 1024
        ),
    )(
        frames.reshape(slots * chan * frame_n, cells),
        keep_list[None],
        train_slot[None],
        stem_weight,
        stem_gain[None],
        stem_shift[None],
        mixer_gain[None],
        mixer_shift[None],
        down_bias[None],
        mixer_flat,
        down_weight,
    )
    return out.reshape(clips, frame_n // 2, row_n // 2, COLS // 2, chan_out)


def solution(mesh):
    return jax.shard_map(
        local,
        mesh=mesh,
        in_specs=(
            P("clip", None, "tm", "row"),
            P("clip"),
            P(),
            P(),
            P(),
            P(),
            P(),
            P(),
            P(),
            P(),
            P(),
        ),
        out_specs=P("clip", "tm", "row", None, None),
        check_vma=False,
    )
```

```python
import functools

import jax
import jax.numpy as jnp
from jax import lax
from jax.experimental import pallas as pl
from jax.experimental.pallas import tpu as pltpu
from jax.sharding import PartitionSpec as P

GROUPS = 32
COLS = 64
HALO = 2
TAPS = 3
MESH = pl.DeviceIdType.MESH
F32 = jnp.float32
BF16 = jnp.bfloat16

eps = 1e-06


def iota(shape, dim):
    return lax.broadcasted_iota(jnp.int32, shape, dim)


def quot(value, by):
    return lax.shift_right_logical(value * (65536 // by + 1), 16)


def rest(value, by):
    return value - quot(value, by) * by


def dot(left, right):
    return jnp.dot(left, right, preferred_element_type=F32)


def silu(value):
    half = value * 0.5
    return half + half * jnp.tanh(half)


def one_hot(flag):
    return jnp.where(flag, 1.0, 0.0).astype(BF16)


def kernel(
    sizes,
    frames_hbm,
    keep_hbm,
    train_hbm,
    stem_w_hbm,
    stem_gain_hbm,
    stem_shift_hbm,
    mixer_w_hbm,
    mixer_gain_hbm,
    mixer_shift_hbm,
    down_w_hbm,
    down_bias_hbm,
    out_ref,
    frames_ref,
    keep_ref,
    train_ref,
    stem_w_ref,
    stem_gain_ref,
    stem_shift_ref,
    mixer_w,
    mixer_gain_ref,
    mixer_shift_ref,
    down_w,
    down_bias_ref,
    packed,
    landed,
    stem_scr,
    hidden_scr,
    mixer_scr,
    sums1,
    sums2,
    load_sem,
    frame_send,
    frame_recv,
    sum_send,
    sum_recv,
):
    clip_n, row_dev, time_dev, clips, chan, frame_n, row_n, rounds = sizes
    cells = row_n * COLS
    c = lax.axis_index("clip")
    r = lax.axis_index("row")
    t = lax.axis_index("tm")
    me = r * time_dev + t
    peers = row_dev * time_dev
    per_clip = frame_n * chan
    halo_cells = HALO * COLS
    wide = cells + 2 * halo_cells
    out_cells = cells + 2 * COLS
    ext_f = frame_n + HALO
    chan_mid = stem_w_ref.shape[1]
    chan_out = mixer_w.shape[1]

    loads = [
        pltpu.make_async_copy(source, target, load_sem.at[number])
        for number, (source, target) in enumerate(
            (
                (frames_hbm, frames_ref),
                (keep_hbm, keep_ref),
                (train_hbm, train_ref),
                (stem_w_hbm, stem_w_ref),
                (stem_gain_hbm, stem_gain_ref),
                (stem_shift_hbm, stem_shift_ref),
                (mixer_w_hbm, mixer_w),
                (mixer_gain_hbm, mixer_gain_ref),
                (mixer_shift_hbm, mixer_shift_ref),
                (down_w_hbm, down_w),
                (down_bias_hbm, down_bias_ref),
            )
        )
    ]
    for load in loads:
        load.start()

    landed[...] = jnp.zeros_like(landed)

    barrier = pltpu.get_barrier_semaphore()
    for j in range(1, peers):
        other = lax.rem(me + j, peers)
        pl.semaphore_signal(
            barrier,
            inc=1,
            device_id={"row": other // time_dev, "tm": lax.rem(other, time_dev)},
            device_id_type=MESH,
        )
    rows_near = 1 + (r > 0).astype(jnp.int32) + (r < row_dev - 1).astype(jnp.int32)
    times_near = 1 + (t > 0).astype(jnp.int32) + (t < time_dev - 1).astype(jnp.int32)
    for k in range(1, clip_n):
        for dr in (-1, 0, 1):
            for dt in (-1, 0, 1):

                @pl.when((r + dr >= 0) & (r + dr < row_dev) & (t + dt >= 0) & (t + dt < time_dev))
                def _():
                    pl.semaphore_signal(
                        barrier,
                        inc=1,
                        device_id={"clip": lax.rem(c + k, clip_n), "row": r + dr, "tm": t + dt},
                        device_id_type=MESH,
                    )

    for load in loads[:3]:
        load.wait()

    slot_n = keep_ref.shape[1]
    enc_n = train_ref.shape[1]
    rows_in = slot_n * per_clip
    rows_out = enc_n * per_clip
    named = one_hot(iota((enc_n, slot_n), 0) == keep_ref[...])
    spread = one_hot(quot(iota((slot_n, rows_in), 1), per_clip) == iota((slot_n, rows_in), 0))
    by_row = dot(named, spread).astype(BF16)
    wanted = one_hot(quot(iota((rows_out, enc_n), 0), per_clip) == train_ref[...])
    chosen = dot(wanted, by_row)
    row_at = rest(iota((rows_out, rows_in), 0), per_clip)
    col_at = rest(iota((rows_out, rows_in), 1), per_clip)
    same = (quot(row_at, chan) == rest(col_at, frame_n)) & (
        rest(row_at, chan) == quot(col_at, frame_n)
    )
    chosen = jnp.where(same, chosen, 0.0).astype(BF16)
    flat_frames = jnp.concatenate(
        [frames_ref[s, i].astype(F32) for s in range(slot_n) for i in range(chan)], axis=0
    ).astype(BF16)
    picked = dot(chosen, flat_frames).astype(BF16)
    packed[...] = picked.reshape(packed.shape)

    pl.semaphore_wait(barrier, peers - 1 + (clip_n - 1) * rows_near * times_near)

    def frame_copy(k, dt, dr):
        if dr == 0:
            src, dst = pl.ds(0, cells), pl.ds(halo_cells, cells)
        elif dr == 1:
            src, dst = pl.ds(cells - halo_cells, halo_cells), pl.ds(0, halo_cells)
        else:
            src, dst = pl.ds(0, halo_cells), pl.ds(halo_cells + cells, halo_cells)
        goal = lax.rem(c + k, clip_n)
        return pltpu.make_async_remote_copy(
            src_ref=packed.at[goal, :, src],
            dst_ref=landed.at[k, dt, :, dst],
            send_sem=frame_send.at[k, dt, dr + 1],
            recv_sem=frame_recv.at[k, dt, dr + 1],
            device_id={"clip": goal, "row": r + dr, "tm": t + dt},
            device_id_type=MESH,
        )

    moves = [
        (k, dt, dr)
        for k in range(clip_n - 1, -1, -1)
        for dt in (1, 0)
        for dr in (1, -1, 0)
        if (k, dt, dr) != (0, 0, 0)
    ]

    def each_move(sign, act):
        for k, dt, dr in moves:
            rr, tt = r + sign * dr, t + sign * dt
            if dr == 0 and dt == 0:
                act(frame_copy(k, dt, dr))
                continue

            @pl.when((rr >= 0) & (rr < row_dev) & (tt >= 0) & (tt < time_dev))
            def _():
                act(frame_copy(k, dt, dr))

    each_move(1, lambda copy: copy.start())
    landed[0, 0, :, halo_cells : halo_cells + cells] = packed[c]

    frames_wide = 2 * frame_n
    lines = frames_wide * chan
    depth = 256
    loads[3].wait()
    stem_w = stem_w_ref[...]
    taps_n = stem_w.shape[0]
    at = iota((depth, taps_n), 0)
    shift_at = quot(at, lines)
    in_shift = rest(at, lines)
    frame_at = quot(in_shift, chan)
    chan_at = in_shift - frame_at * chan
    tap_at = iota((depth, taps_n), 1)
    columns = []
    for f in range(ext_f):
        a = frame_at - f
        index = (a * (TAPS * TAPS) + shift_at) * chan + chan_at
        ok = (a >= 0) & (a < TAPS) & (at < TAPS * TAPS * lines) & (index == tap_at)
        columns.append(dot(one_hot(ok), stem_w).astype(BF16))
    stem_big = jnp.concatenate(columns, axis=1)

    lane = iota((128, 128), 1)
    source = iota((128, 128), 0)
    in_row = lane & (COLS - 1)
    col = 2 * (in_row & (COLS // 2 - 1)) + jnp.where(in_row >= COLS // 2, 1, 0)
    tables = []
    for tap in range(TAPS):
        moved = col + (tap - 1)
        ok = (moved >= 0) & (moved < COLS) & (source == (lane - in_row) + moved)
        tables.append(one_hot(ok))
    col_table = jnp.concatenate(tables, axis=1)

    half_rows = clips * per_clip
    total_rows = 2 * half_rows
    row_at = iota((total_rows, total_rows), 0)
    clip_at = quot(row_at, lines)
    in_clip = rest(row_at, lines)
    frame_at = quot(in_clip, chan)
    chan_at = in_clip - frame_at * chan
    base = clip_at * per_clip + chan_at
    before = jnp.where(t > 0, half_rows + base + frame_at * chan, base)
    goal = jnp.where(frame_at >= frame_n, base + (frame_at - frame_n) * chan, before)
    order = one_hot(goal == iota((total_rows, total_rows), 1))

    each_move(-1, lambda copy: copy.wait_recv())

    volume = landed[0].astype(F32)
    for k in range(1, clip_n):
        volume = volume + landed[k].astype(F32)
    volume = volume.astype(BF16).reshape(total_rows, wide)
    volume = dot(order, volume).astype(BF16)
    blocks = wide // 128
    stacked = jnp.concatenate(
        [volume[:, b * 128 : (b + 1) * 128] for b in range(blocks)], axis=0
    )
    shifted = dot(stacked, col_table)
    views = []
    by_tap = []
    for tap in range(TAPS):
        by_tap.append(
            jnp.concatenate(
                [
                    shifted[b * total_rows : (b + 1) * total_rows, tap * 128 : (tap + 1) * 128]
                    for b in range(blocks)
                ],
                axis=1,
            )
        )
    for row_tap in range(TAPS):
        for tap in range(TAPS):
            if row_tap % 2:
                views.append(
                    pltpu.roll(by_tap[tap], wide - row_tap * COLS, 1)[:, :out_cells]
                )
            else:
                views.append(by_tap[tap][:, row_tap * COLS : row_tap * COLS + out_cells])
    filler = jnp.zeros((depth - TAPS * TAPS * lines, out_cells), F32)

    def sum_copy(buffer, number, index, j):
        other = lax.rem(me + j, peers)
        return pltpu.make_async_remote_copy(
            src_ref=buffer.at[index, me],
            dst_ref=buffer.at[index, me],
            send_sem=sum_send.at[number, j],
            recv_sem=sum_recv.at[number, j],
            device_id={"row": other // time_dev, "tm": lax.rem(other, time_dev)},
            device_id_type=MESH,
        )

    def send_sums(buffer, number, index):
        for j in range(1, peers):
            sum_copy(buffer, number, index, j).start()

    def take_sums(buffer, number, index, gain, shift):
        for j in range(1, peers):
            sum_copy(buffer, number, index, j).wait_recv()
        total = buffer[index, 0]
        for j in range(1, peers):
            total = total + buffer[index, j]
        chan_n = total.shape[1]
        per_group = chan_n // GROUPS
        joined = jnp.where(
            quot(iota((chan_n, chan_n), 0), per_group) == quot(iota((chan_n, chan_n), 1), per_group),
            1.0,
            0.0,
        )
        total = jnp.dot(
            total, joined, preferred_element_type=F32, precision=lax.Precision.HIGHEST
        )
        count = peers * frame_n * cells * per_group
        total = total * (1.0 / count)
        half = total.shape[0] // 2
        mean = total[:half]
        inverse = lax.rsqrt(total[half:] - mean * mean + eps)
        scale = inverse * gain
        return scale, shift - mean * scale

    per_round = clips // rounds
    for turn in range(rounds):
        for pos in range(per_round):
            k = turn * per_round + pos
            patches = jnp.concatenate(
                [view[k * lines : (k + 1) * lines] for view in views] + [filler], axis=0
            ).astype(BF16)
            stem = lax.dot_general(
                patches, stem_big, (((0,), (0,)), ((), ())), preferred_element_type=F32
            )
            stem_scr[k] = stem
            own = stem[COLS : COLS + cells, HALO * chan_mid :]
            values = jnp.sum(own, axis=0, keepdims=True)
            squares = jnp.sum(own * own, axis=0, keepdims=True)
            value_sum = values[:, :chan_mid]
            square_sum = squares[:, :chan_mid]
            for f in range(1, frame_n):
                value_sum = value_sum + values[:, f * chan_mid : (f + 1) * chan_mid]
                square_sum = square_sum + squares[:, f * chan_mid : (f + 1) * chan_mid]
            sums1[turn, me, pos : pos + 1, :] = value_sum
            sums1[turn, me, per_round + pos : per_round + pos + 1, :] = square_sum
        send_sums(sums1, turn, turn)

    top = jnp.where(r > 0, 1.0, 0.0).astype(F32)
    bottom = jnp.where(r < row_dev - 1, 1.0, 0.0).astype(F32)
    ext_rows = row_n + 2
    half_cols = COLS // 2
    x_at = iota((ext_rows * half_cols, chan_mid), 0) & (half_cols - 1)

    def norm_first(k, scale, shift):
        for f in range(ext_f):
            value = stem_scr[k, :, f * chan_mid : (f + 1) * chan_mid]
            value = silu(value * scale + shift)
            value = jnp.concatenate(
                [
                    value[:COLS] * top,
                    value[COLS : COLS + cells],
                    value[COLS + cells :] * bottom,
                ],
                axis=0,
            )
            parts = value.reshape(ext_rows, 2, half_cols, chan_mid)
            even, odd = parts[:, 0], parts[:, 1]
            flat = (ext_rows * half_cols, chan_mid)
            left = jnp.where(x_at == 0, 0.0, pltpu.roll(odd.reshape(flat), 1, 0))
            right = jnp.where(
                x_at == half_cols - 1, 0.0, pltpu.roll(even.reshape(flat), flat[0] - 1, 0)
            )
            left = left.reshape(even.shape)
            right = right.reshape(even.shape)
            before = jnp.stack([left, even], axis=1).reshape(value.shape)
            after = jnp.stack([odd, right], axis=1).reshape(value.shape)
            hidden_scr[k, f, :, :chan_mid] = before.astype(BF16)
            hidden_scr[k, f, :, chan_mid : 2 * chan_mid] = value.astype(BF16)
            hidden_scr[k, f, :, 2 * chan_mid :] = after.astype(BF16)

    def mix(k, turn, pos):
        strip = jnp.concatenate(
            [
                hidden_scr[k, a : a + frame_n, b * COLS : b * COLS + cells, :].reshape(
                    frame_n * cells, TAPS * chan_mid
                )
                for a in range(TAPS)
                for b in range(TAPS)
            ],
            axis=1,
        )
        mixed = dot(strip, mixer_w[...])
        mixer_scr[k] = mixed.reshape(frame_n, cells, chan_out)
        value_sum = jnp.sum(mixed, axis=0, keepdims=True)
        square_sum = jnp.sum(mixed * mixed, axis=0, keepdims=True)
        sums2[turn, me, pos : pos + 1, :] = value_sum
        sums2[turn, me, per_round + pos : per_round + pos + 1, :] = square_sum

    for load in loads[4:7]:
        load.wait()
    for turn in range(rounds):
        scale, shift = take_sums(sums1, turn, turn, stem_gain_ref[...], stem_shift_ref[...])
        for pos in range(per_round):
            k = turn * per_round + pos
            norm_first(k, scale[pos : pos + 1], shift[pos : pos + 1])
            mix(k, turn, pos)
        send_sums(sums2, rounds + turn, turn)

    for load in loads[7:]:
        load.wait()
    bias = down_bias_ref[...]
    pairs = frame_n // 2
    out_rows = row_n // 2
    for turn in range(rounds):
        scale, shift = take_sums(
            sums2, rounds + turn, turn, mixer_gain_ref[...], mixer_shift_ref[...]
        )
        for pos in range(per_round):
            k = turn * per_round + pos
            squares = []
            for pair in range(pairs):
                acts = []
                for f in (2 * pair, 2 * pair + 1):
                    value = mixer_scr[k, f] * scale[pos : pos + 1] + shift[pos : pos + 1]
                    acts.append(silu(value).astype(BF16).astype(F32))
                pooled = ((acts[0] + acts[1]) * 0.5).astype(BF16)
                pooled = pooled.reshape(out_rows, 2, 2, half_cols, chan_out)
                squares.append(
                    jnp.concatenate(
                        [
                            pooled[:, p, q].reshape(out_rows * half_cols, chan_out)
                            for p in range(2)
                            for q in range(2)
                        ],
                        axis=1,
                    )
                )
            block = jnp.concatenate(squares, axis=0)
            latent = dot(block, down_w[...]) + bias
            size = block.shape[0]
            out_ref[k * size : (k + 1) * size, :] = latent.astype(BF16)

    each_move(1, lambda copy: copy.wait_send())
    for turn in range(rounds):
        for j in range(1, peers):
            sum_copy(sums1, turn, turn, j).wait_send()
            sum_copy(sums2, rounds + turn, turn, j).wait_send()


def local(
    frames,
    keep_list,
    train_slot,
    stem_weight,
    stem_gain,
    stem_shift,
    mixer_weight,
    mixer_gain,
    mixer_shift,
    down_weight,
    down_bias,
):
    clip_n = lax.axis_size("clip")
    row_dev = lax.axis_size("row")
    time_dev = lax.axis_size("tm")
    slots, chan, frame_n, cells = frames.shape
    clips = train_slot.shape[0] // clip_n
    row_n = cells // COLS
    chan_mid = stem_weight.shape[1]
    chan_out = mixer_weight.shape[3]
    rounds = 2 if clips % 2 == 0 else 1
    per_round = clips // rounds
    peers = row_dev * time_dev
    ext_f = frame_n + HALO
    out_cells = cells + 2 * COLS
    sizes = (clip_n, row_dev, time_dev, clips, chan, frame_n, row_n, rounds)
    out_rows = clips * (frame_n // 2) * (row_n // 2) * (COLS // 2)
    operands = (
        frames,
        keep_list[None],
        train_slot[None],
        stem_weight,
        stem_gain[None],
        stem_shift[None],
        mixer_weight.reshape(-1, chan_out),
        mixer_gain[None],
        mixer_shift[None],
        down_weight,
        down_bias[None],
    )
    vmem = pl.BlockSpec(memory_space=pltpu.VMEM)
    hbm = pl.BlockSpec(memory_space=pl.ANY)
    out = pl.pallas_call(
        functools.partial(kernel, sizes),
        out_shape=jax.ShapeDtypeStruct((out_rows, chan_out), BF16),
        in_specs=[hbm] * len(operands),
        out_specs=vmem,
        scratch_shapes=[pltpu.VMEM(operand.shape, operand.dtype) for operand in operands]
        + [
            pltpu.VMEM((clip_n, clips * frame_n * chan, cells), BF16),
            pltpu.VMEM((clip_n, 2, clips * frame_n * chan, cells + 2 * HALO * COLS), BF16),
            pltpu.VMEM((clips, out_cells, ext_f * chan_mid), F32),
            pltpu.VMEM((clips, ext_f, out_cells, TAPS * chan_mid), BF16),
            pltpu.VMEM((clips, frame_n, cells, chan_out), F32),
            pltpu.VMEM((rounds, peers, 2 * per_round, chan_mid), F32),
            pltpu.VMEM((rounds, peers, 2 * per_round, chan_out), F32),
            pltpu.SemaphoreType.DMA((len(operands),)),
            pltpu.SemaphoreType.DMA((clip_n, 2, 3)),
            pltpu.SemaphoreType.DMA((clip_n, 2, 3)),
            pltpu.SemaphoreType.DMA((2 * rounds, peers)),
            pltpu.SemaphoreType.DMA((2 * rounds, peers)),
        ],
        compiler_params=pltpu.CompilerParams(
            collective_id=0, has_side_effects=True, vmem_limit_bytes=64 * 1024 * 1024
        ),
    )(*operands)
    return out.reshape(clips, frame_n // 2, row_n // 2, COLS // 2, chan_out)


def solution(mesh):
    return jax.shard_map(
        local,
        mesh=mesh,
        in_specs=(
            P("clip", None, "tm", "row"),
            P("clip"),
            P(),
            P(),
            P(),
            P(),
            P(),
            P(),
            P(),
            P(),
            P(),
        ),
        out_specs=P("clip", "tm", "row", None, None),
        check_vma=False,
    )
```

```python
import functools

import jax
import jax.numpy as jnp
from jax import lax
from jax.experimental import pallas as pl
from jax.experimental.pallas import tpu as pltpu
from jax.sharding import PartitionSpec as P

GROUPS = 32
COLS = 64
HALO = 2
TAPS = 3
MESH = pl.DeviceIdType.MESH
F32 = jnp.float32
BF16 = jnp.bfloat16

eps = 1e-06


def iota(shape, dim):
    return lax.broadcasted_iota(jnp.int32, shape, dim)


def quot(value, by):
    return lax.shift_right_logical(value * (65536 // by + 1), 16)


def rest(value, by):
    return value - quot(value, by) * by


def dot(left, right):
    return jnp.dot(left, right, preferred_element_type=F32)


def silu(value):
    half = value * 0.5
    return half + half * jnp.tanh(half)


def one_hot(flag):
    return jnp.where(flag, 1.0, 0.0).astype(BF16)


def kernel(
    sizes,
    frames_hbm,
    keep_hbm,
    train_hbm,
    stem_w_hbm,
    stem_gain_hbm,
    stem_shift_hbm,
    mixer_w_hbm,
    mixer_gain_hbm,
    mixer_shift_hbm,
    down_w_hbm,
    down_bias_hbm,
    out_ref,
    frames_ref,
    keep_ref,
    train_ref,
    stem_w_ref,
    stem_gain_ref,
    stem_shift_ref,
    mixer_w,
    mixer_gain_ref,
    mixer_shift_ref,
    down_w,
    down_bias_ref,
    packed,
    landed,
    stem_scr,
    hidden_scr,
    mixer_scr,
    load_sem,
    frame_send,
    frame_recv,
    sum_send,
    sum_recv,
    *sums,
):
    clip_n, row_dev, time_dev, clips, chan, frame_n, row_n, rounds1, rounds2 = sizes
    cells = row_n * COLS
    c = lax.axis_index("clip")
    r = lax.axis_index("row")
    t = lax.axis_index("tm")
    me = r * time_dev + t
    peers = row_dev * time_dev
    per_clip = frame_n * chan
    halo_cells = HALO * COLS
    wide = cells + 2 * halo_cells
    out_cells = cells + 2 * COLS
    ext_f = frame_n + HALO
    chan_mid = stem_w_ref.shape[1]
    chan_out = mixer_w.shape[1]

    loads = [
        pltpu.make_async_copy(source, target, load_sem.at[number])
        for number, (source, target) in enumerate(
            (
                (frames_hbm, frames_ref),
                (keep_hbm, keep_ref),
                (train_hbm, train_ref),
                (stem_w_hbm, stem_w_ref),
                (stem_gain_hbm, stem_gain_ref),
                (stem_shift_hbm, stem_shift_ref),
                (mixer_w_hbm, mixer_w),
                (mixer_gain_hbm, mixer_gain_ref),
                (mixer_shift_hbm, mixer_shift_ref),
                (down_w_hbm, down_w),
                (down_bias_hbm, down_bias_ref),
            )
        )
    ]
    for load in loads:
        load.start()

    landed[...] = jnp.zeros_like(landed)

    barrier = pltpu.get_barrier_semaphore()
    for j in range(1, peers):
        other = lax.rem(me + j, peers)
        pl.semaphore_signal(
            barrier,
            inc=1,
            device_id={"row": other // time_dev, "tm": lax.rem(other, time_dev)},
            device_id_type=MESH,
        )
    rows_near = 1 + (r > 0).astype(jnp.int32) + (r < row_dev - 1).astype(jnp.int32)
    times_near = 1 + (t > 0).astype(jnp.int32) + (t < time_dev - 1).astype(jnp.int32)
    for k in range(1, clip_n):
        for dr in (-1, 0, 1):
            for dt in (-1, 0, 1):

                @pl.when((r + dr >= 0) & (r + dr < row_dev) & (t + dt >= 0) & (t + dt < time_dev))
                def _():
                    pl.semaphore_signal(
                        barrier,
                        inc=1,
                        device_id={"clip": lax.rem(c + k, clip_n), "row": r + dr, "tm": t + dt},
                        device_id_type=MESH,
                    )

    for load in loads[:3]:
        load.wait()

    slot_n = keep_ref.shape[1]
    enc_n = train_ref.shape[1]
    rows_in = slot_n * per_clip
    rows_out = enc_n * per_clip
    named = one_hot(iota((enc_n, slot_n), 0) == keep_ref[...])
    spread = one_hot(quot(iota((slot_n, rows_in), 1), per_clip) == iota((slot_n, rows_in), 0))
    by_row = dot(named, spread).astype(BF16)
    wanted = one_hot(quot(iota((rows_out, enc_n), 0), per_clip) == train_ref[...])
    chosen = dot(wanted, by_row)
    row_at = rest(iota((rows_out, rows_in), 0), per_clip)
    col_at = rest(iota((rows_out, rows_in), 1), per_clip)
    same = (quot(row_at, chan) == rest(col_at, frame_n)) & (
        rest(row_at, chan) == quot(col_at, frame_n)
    )
    chosen = jnp.where(same, chosen, 0.0).astype(BF16)
    flat_frames = jnp.concatenate(
        [frames_ref[s, i].astype(F32) for s in range(slot_n) for i in range(chan)], axis=0
    ).astype(BF16)
    picked = dot(chosen, flat_frames).astype(BF16)
    packed[...] = picked.reshape(packed.shape)

    pl.semaphore_wait(barrier, peers - 1 + (clip_n - 1) * rows_near * times_near)

    def frame_copy(k, dt, dr):
        if dr == 0:
            src, dst = pl.ds(0, cells), pl.ds(halo_cells, cells)
        elif dr == 1:
            src, dst = pl.ds(cells - halo_cells, halo_cells), pl.ds(0, halo_cells)
        else:
            src, dst = pl.ds(0, halo_cells), pl.ds(halo_cells + cells, halo_cells)
        goal = lax.rem(c + k, clip_n)
        return pltpu.make_async_remote_copy(
            src_ref=packed.at[goal, :, src],
            dst_ref=landed.at[k, dt, :, dst],
            send_sem=frame_send.at[k, dt, dr + 1],
            recv_sem=frame_recv.at[k, dt, dr + 1],
            device_id={"clip": goal, "row": r + dr, "tm": t + dt},
            device_id_type=MESH,
        )

    moves = [
        (k, dt, dr)
        for k in range(clip_n - 1, -1, -1)
        for dt in (1, 0)
        for dr in (1, -1, 0)
        if (k, dt, dr) != (0, 0, 0)
    ]

    def each_move(sign, act):
        for k, dt, dr in moves:
            rr, tt = r + sign * dr, t + sign * dt
            if dr == 0 and dt == 0:
                act(frame_copy(k, dt, dr))
                continue

            @pl.when((rr >= 0) & (rr < row_dev) & (tt >= 0) & (tt < time_dev))
            def _():
                act(frame_copy(k, dt, dr))

    each_move(1, lambda copy: copy.start())
    landed[0, 0, :, halo_cells : halo_cells + cells] = packed[c]

    frames_wide = 2 * frame_n
    lines = frames_wide * chan
    depth = 256
    loads[3].wait()
    stem_w = stem_w_ref[...]
    taps_n = stem_w.shape[0]
    at = iota((depth, taps_n), 0)
    shift_at = quot(at, lines)
    in_shift = rest(at, lines)
    frame_at = quot(in_shift, chan)
    chan_at = in_shift - frame_at * chan
    tap_at = iota((depth, taps_n), 1)
    columns = []
    for f in range(ext_f):
        a = frame_at - f
        index = (a * (TAPS * TAPS) + shift_at) * chan + chan_at
        ok = (a >= 0) & (a < TAPS) & (at < TAPS * TAPS * lines) & (index == tap_at)
        columns.append(dot(one_hot(ok), stem_w).astype(BF16))
    stem_big = jnp.concatenate(columns, axis=1)

    lane = iota((128, 128), 1)
    source = iota((128, 128), 0)
    in_row = lane & (COLS - 1)
    col = 2 * (in_row & (COLS // 2 - 1)) + jnp.where(in_row >= COLS // 2, 1, 0)
    tables = []
    for tap in range(TAPS):
        moved = col + (tap - 1)
        ok = (moved >= 0) & (moved < COLS) & (source == (lane - in_row) + moved)
        tables.append(one_hot(ok))
    col_table = jnp.concatenate(tables, axis=1)

    half_rows = clips * per_clip
    total_rows = 2 * half_rows
    row_at = iota((total_rows, total_rows), 0)
    clip_at = quot(row_at, lines)
    in_clip = rest(row_at, lines)
    frame_at = quot(in_clip, chan)
    chan_at = in_clip - frame_at * chan
    base = clip_at * per_clip + chan_at
    before = jnp.where(t > 0, half_rows + base + frame_at * chan, base)
    goal = jnp.where(frame_at >= frame_n, base + (frame_at - frame_n) * chan, before)
    order = one_hot(goal == iota((total_rows, total_rows), 1))

    def group_table(chan_n):
        per_group = chan_n // GROUPS
        group_at = quot(iota((chan_n, chan_n), 0), per_group)
        return one_hot(group_at == quot(iota((chan_n, chan_n), 1), per_group))

    joined_mid, joined_out = group_table(chan_mid), group_table(chan_out)

    each_move(-1, lambda copy: copy.wait_recv())

    volume = landed[0].astype(F32)
    for k in range(1, clip_n):
        volume = volume + landed[k].astype(F32)
    volume = volume.astype(BF16).reshape(total_rows, wide)
    volume = dot(order, volume).astype(BF16)
    blocks = wide // 128
    stacked = jnp.concatenate(
        [volume[:, b * 128 : (b + 1) * 128] for b in range(blocks)], axis=0
    )
    shifted = dot(stacked, col_table)
    views = []
    by_tap = []
    for tap in range(TAPS):
        by_tap.append(
            jnp.concatenate(
                [
                    shifted[b * total_rows : (b + 1) * total_rows, tap * 128 : (tap + 1) * 128]
                    for b in range(blocks)
                ],
                axis=1,
            )
        )
    for row_tap in range(TAPS):
        for tap in range(TAPS):
            if row_tap % 2:
                views.append(
                    pltpu.roll(by_tap[tap], wide - row_tap * COLS, 1)[:, :out_cells]
                )
            else:
                views.append(by_tap[tap][:, row_tap * COLS : row_tap * COLS + out_cells])
    filler = jnp.zeros((depth - TAPS * TAPS * lines, out_cells), F32)

    def sum_copy(number, j):
        other = lax.rem(me + j, peers)
        return pltpu.make_async_remote_copy(
            src_ref=sums[number].at[0],
            dst_ref=sums[number].at[j],
            send_sem=sum_send.at[number],
            recv_sem=sum_recv.at[number],
            device_id={"row": other // time_dev, "tm": lax.rem(other, time_dev)},
            device_id_type=MESH,
        )

    def sum_wait(number, semaphore):
        others = sums[number].at[pl.ds(1, peers - 1)]
        pltpu.make_async_copy(others, others, semaphore.at[number]).wait()

    def send_sums(number, clip_sums):
        for place, (value_sum, square_sum) in enumerate(clip_sums):
            low = len(clip_sums) + place
            sums[number][0, place : place + 1, :] = value_sum
            sums[number][0, low : low + 1, :] = square_sum
        for j in range(1, peers):
            sum_copy(number, j).start()

    def take_sums(number, joined, gain, shift):
        sum_wait(number, sum_recv)
        total = sums[number][0]
        for j in range(1, peers):
            total = total + sums[number][j]
        rows = total.shape[0]
        high = total.astype(BF16).astype(F32)
        middle = (total - high).astype(BF16).astype(F32)
        low = total - high - middle
        joint = dot(jnp.concatenate([high, middle, low], axis=0).astype(BF16), joined)
        total = joint[:rows] + joint[rows : 2 * rows] + joint[2 * rows :]
        per_group = total.shape[1] // GROUPS
        total = total * (1.0 / (peers * frame_n * cells * per_group))
        mean = total[: rows // 2]
        inverse = lax.rsqrt(total[rows // 2 :] - mean * mean + eps)
        scale = inverse * gain
        move = shift - mean * scale
        return [(scale[i : i + 1], move[i : i + 1]) for i in range(rows // 2)]

    for number, group in enumerate(rounds1):
        clip_sums = []
        for k in group:
            patches = jnp.concatenate(
                [view[k * lines : (k + 1) * lines] for view in views] + [filler], axis=0
            ).astype(BF16)
            stem = lax.dot_general(
                patches, stem_big, (((0,), (0,)), ((), ())), preferred_element_type=F32
            )
            stem_scr[k] = stem
            own = stem[COLS : COLS + cells, HALO * chan_mid :]
            values = jnp.sum(own, axis=0, keepdims=True)
            squares = jnp.sum(own * own, axis=0, keepdims=True)
            value_sum = values[:, :chan_mid]
            square_sum = squares[:, :chan_mid]
            for f in range(1, frame_n):
                value_sum = value_sum + values[:, f * chan_mid : (f + 1) * chan_mid]
                square_sum = square_sum + squares[:, f * chan_mid : (f + 1) * chan_mid]
            clip_sums.append((value_sum, square_sum))
        send_sums(number, clip_sums)

    top = jnp.where(r > 0, 1.0, 0.0).astype(F32)
    bottom = jnp.where(r < row_dev - 1, 1.0, 0.0).astype(F32)
    ext_rows = row_n + 2
    half_cols = COLS // 2
    x_at = iota((ext_rows * half_cols, chan_mid), 0) & (half_cols - 1)

    def norm_first(k, frames_at, scale, shift):
        for f in frames_at:
            value = stem_scr[k, :, f * chan_mid : (f + 1) * chan_mid]
            value = silu(value * scale + shift)
            value = jnp.concatenate(
                [
                    value[:COLS] * top,
                    value[COLS : COLS + cells],
                    value[COLS + cells :] * bottom,
                ],
                axis=0,
            )
            parts = value.reshape(ext_rows, 2, half_cols, chan_mid)
            even, odd = parts[:, 0], parts[:, 1]
            flat = (ext_rows * half_cols, chan_mid)
            left = jnp.where(x_at == 0, 0.0, pltpu.roll(odd.reshape(flat), 1, 0))
            right = jnp.where(
                x_at == half_cols - 1, 0.0, pltpu.roll(even.reshape(flat), flat[0] - 1, 0)
            )
            left = left.reshape(even.shape)
            right = right.reshape(even.shape)
            before = jnp.stack([left, even], axis=1).reshape(value.shape)
            after = jnp.stack([odd, right], axis=1).reshape(value.shape)
            hidden_scr[k, f, :, :chan_mid] = before.astype(BF16)
            hidden_scr[k, f, :, chan_mid : 2 * chan_mid] = value.astype(BF16)
            hidden_scr[k, f, :, 2 * chan_mid :] = after.astype(BF16)

    def mix(k, first, count):
        strip = jnp.concatenate(
            [
                hidden_scr[k, first + a : first + a + count, b * COLS : b * COLS + cells, :].reshape(
                    count * cells, TAPS * chan_mid
                )
                for a in range(TAPS)
                for b in range(TAPS)
            ],
            axis=1,
        )
        mixed = dot(strip, mixer_w[...])
        mixer_scr[k, first : first + count] = mixed.reshape(count, cells, chan_out)
        return (
            jnp.sum(mixed, axis=0, keepdims=True),
            jnp.sum(mixed * mixed, axis=0, keepdims=True),
        )

    for load in loads[4:7]:
        load.wait()
    norms = {}

    def take_first(number):
        taken = take_sums(number, joined_mid, stem_gain_ref[...], stem_shift_ref[...])
        norms.update(zip(rounds1[number], taken))

    take_first(0)
    norm_first(0, range(ext_f), *norms[0])
    half = frame_n // 2
    done = []
    for k in range(clips):
        low_sums = mix(k, 0, half)
        if k + 1 < clips:
            if k + 1 not in norms:
                take_first(1)
            norm_first(k + 1, range(ext_f), *norms[k + 1])
        high_sums = mix(k, half, frame_n - half)
        done.append((low_sums[0] + high_sums[0], low_sums[1] + high_sums[1]))
        for number, group in enumerate(rounds2):
            if group[-1] == k:
                send_sums(len(rounds1) + number, [done[i] for i in group])

    for load in loads[7:]:
        load.wait()
    bias = down_bias_ref[...]
    pairs = frame_n // 2
    out_rows = row_n // 2
    for number, group in enumerate(rounds2):
        taken = take_sums(
            len(rounds1) + number, joined_out, mixer_gain_ref[...], mixer_shift_ref[...]
        )
        for k, (scale, shift) in zip(group, taken):
            squares = []
            for pair in range(pairs):
                acts = []
                for f in (2 * pair, 2 * pair + 1):
                    value = mixer_scr[k, f] * scale + shift
                    acts.append(silu(value).astype(BF16).astype(F32))
                pooled = ((acts[0] + acts[1]) * 0.5).astype(BF16)
                pooled = pooled.reshape(out_rows, 2, 2, half_cols, chan_out)
                squares.append(
                    jnp.concatenate(
                        [
                            pooled[:, p, q].reshape(out_rows * half_cols, chan_out)
                            for p in range(2)
                            for q in range(2)
                        ],
                        axis=1,
                    )
                )
            block = jnp.concatenate(squares, axis=0)
            latent = dot(block, down_w[...]) + bias
            size = block.shape[0]
            out_ref[k * size : (k + 1) * size, :] = latent.astype(BF16)

    each_move(1, lambda copy: copy.wait_send())
    for number in range(len(sums)):
        sum_wait(number, sum_send)


def local(
    frames,
    keep_list,
    train_slot,
    stem_weight,
    stem_gain,
    stem_shift,
    mixer_weight,
    mixer_gain,
    mixer_shift,
    down_weight,
    down_bias,
):
    clip_n = lax.axis_size("clip")
    row_dev = lax.axis_size("row")
    time_dev = lax.axis_size("tm")
    slots, chan, frame_n, cells = frames.shape
    clips = train_slot.shape[0] // clip_n
    row_n = cells // COLS
    chan_mid = stem_weight.shape[1]
    chan_out = mixer_weight.shape[3]
    every = tuple(range(clips))
    rounds1 = tuple(part for part in (every[:1], every[1:]) if part)
    rounds2 = tuple(part for part in (every[:-1], every[-1:]) if part)
    peers = row_dev * time_dev
    ext_f = frame_n + HALO
    out_cells = cells + 2 * COLS
    sizes = (clip_n, row_dev, time_dev, clips, chan, frame_n, row_n, rounds1, rounds2)
    out_rows = clips * (frame_n // 2) * (row_n // 2) * (COLS // 2)
    operands = (
        frames,
        keep_list[None],
        train_slot[None],
        stem_weight,
        stem_gain[None],
        stem_shift[None],
        mixer_weight.reshape(-1, chan_out),
        mixer_gain[None],
        mixer_shift[None],
        down_weight,
        down_bias[None],
    )
    vmem = pl.BlockSpec(memory_space=pltpu.VMEM)
    hbm = pl.BlockSpec(memory_space=pltpu.HBM)
    out = pl.pallas_call(
        functools.partial(kernel, sizes),
        out_shape=jax.ShapeDtypeStruct((out_rows, chan_out), BF16),
        in_specs=[hbm] * len(operands),
        out_specs=vmem,
        scratch_shapes=[pltpu.VMEM(operand.shape, operand.dtype) for operand in operands]
        + [
            pltpu.VMEM((clip_n, clips * frame_n * chan, cells), BF16),
            pltpu.VMEM((clip_n, 2, clips * frame_n * chan, cells + 2 * HALO * COLS), BF16),
            pltpu.VMEM((clips, out_cells, ext_f * chan_mid), F32),
            pltpu.VMEM((clips, ext_f, out_cells, TAPS * chan_mid), BF16),
            pltpu.VMEM((clips, frame_n, cells, chan_out), F32),
            pltpu.SemaphoreType.DMA((len(operands),)),
            pltpu.SemaphoreType.DMA((clip_n, 2, 3)),
            pltpu.SemaphoreType.DMA((clip_n, 2, 3)),
            pltpu.SemaphoreType.DMA((len(rounds1) + len(rounds2),)),
            pltpu.SemaphoreType.DMA((len(rounds1) + len(rounds2),)),
        ]
        + [pltpu.VMEM((peers, 2 * len(part), chan_mid), F32) for part in rounds1]
        + [pltpu.VMEM((peers, 2 * len(part), chan_out), F32) for part in rounds2],
        compiler_params=pltpu.CompilerParams(
            collective_id=0, has_side_effects=True, vmem_limit_bytes=64 * 1024 * 1024
        ),
    )(*operands)
    return out.reshape(clips, frame_n // 2, row_n // 2, COLS // 2, chan_out)


def solution(mesh):
    return jax.shard_map(
        local,
        mesh=mesh,
        in_specs=(
            P("clip", None, "tm", "row"),
            P("clip"),
            P(),
            P(),
            P(),
            P(),
            P(),
            P(),
            P(),
            P(),
            P(),
        ),
        out_specs=P("clip", "tm", "row", None, None),
        check_vma=False,
    )
```

```python
import functools

import jax
import jax.numpy as jnp
from jax import lax
from jax.experimental import pallas as pl
from jax.experimental.pallas import tpu as pltpu
from jax.sharding import PartitionSpec as P

GROUPS = 32
COLS = 64
HALO = 2
TAPS = 3
MESH = pl.DeviceIdType.MESH
F32 = jnp.float32
BF16 = jnp.bfloat16

eps = 1e-06


def iota(shape, dim):
    return lax.broadcasted_iota(jnp.int32, shape, dim)


def quot(value, by):
    return lax.shift_right_logical(value * (65536 // by + 1), 16)


def rest(value, by):
    return value - quot(value, by) * by


def dot(left, right):
    return jnp.dot(left, right, preferred_element_type=F32)


def silu(value):
    half = value * 0.5
    return half + half * jnp.tanh(half)


def one_hot(flag):
    return jnp.where(flag, 1.0, 0.0).astype(BF16)


def kernel(
    sizes,
    frames_hbm,
    keep_hbm,
    train_hbm,
    stem_w_hbm,
    stem_gain_hbm,
    stem_shift_hbm,
    mixer_w_hbm,
    mixer_gain_hbm,
    mixer_shift_hbm,
    down_w_hbm,
    down_bias_hbm,
    out_ref,
    frames_ref,
    keep_ref,
    train_ref,
    stem_w_ref,
    stem_gain_ref,
    stem_shift_ref,
    mixer_w,
    mixer_gain_ref,
    mixer_shift_ref,
    down_w,
    down_bias_ref,
    packed,
    landed,
    stem_scr,
    hidden_scr,
    mixer_scr,
    view_scr,
    own1,
    own2,
    norm1,
    norm2,
    load_sem,
    frame_send,
    frame_recv,
    sum_send,
    sum_recv,
    *sums,
):
    clip_n, row_dev, time_dev, clips, chan, frame_n, row_n, rounds1, rounds2 = sizes
    cells = row_n * COLS
    c = lax.axis_index("clip")
    r = lax.axis_index("row")
    t = lax.axis_index("tm")
    me = r * time_dev + t
    peers = row_dev * time_dev
    per_clip = frame_n * chan
    halo_cells = HALO * COLS
    wide = cells + 2 * halo_cells
    out_cells = cells + 2 * COLS
    ext_f = frame_n + HALO
    chan_mid = stem_w_ref.shape[1]
    chan_out = mixer_w.shape[1]

    loads = [
        pltpu.make_async_copy(source, target, load_sem.at[number])
        for number, (source, target) in enumerate(
            (
                (frames_hbm, frames_ref),
                (keep_hbm, keep_ref),
                (train_hbm, train_ref),
                (stem_w_hbm, stem_w_ref),
                (stem_gain_hbm, stem_gain_ref),
                (stem_shift_hbm, stem_shift_ref),
                (mixer_w_hbm, mixer_w),
                (mixer_gain_hbm, mixer_gain_ref),
                (mixer_shift_hbm, mixer_shift_ref),
                (down_w_hbm, down_w),
                (down_bias_hbm, down_bias_ref),
            )
        )
    ]
    for load in loads:
        load.start()

    landed[...] = jnp.zeros_like(landed)

    barrier = pltpu.get_barrier_semaphore()

    @pl.loop(1, peers)
    def _(j):
        other = lax.rem(me + j, peers)
        pl.semaphore_signal(
            barrier,
            inc=1,
            device_id={"row": other // time_dev, "tm": lax.rem(other, time_dev)},
            device_id_type=MESH,
        )

    rows_near = 1 + (r > 0).astype(jnp.int32) + (r < row_dev - 1).astype(jnp.int32)
    times_near = 1 + (t > 0).astype(jnp.int32) + (t < time_dev - 1).astype(jnp.int32)
    for k in range(1, clip_n):
        for dr in (-1, 0, 1):
            for dt in (-1, 0, 1):

                @pl.when((r + dr >= 0) & (r + dr < row_dev) & (t + dt >= 0) & (t + dt < time_dev))
                def _():
                    pl.semaphore_signal(
                        barrier,
                        inc=1,
                        device_id={"clip": lax.rem(c + k, clip_n), "row": r + dr, "tm": t + dt},
                        device_id_type=MESH,
                    )

    for load in loads[:3]:
        load.wait()

    slot_n = keep_ref.shape[1]
    enc_n = train_ref.shape[1]
    rows_in = slot_n * per_clip
    rows_out = enc_n * per_clip
    named = one_hot(iota((enc_n, slot_n), 0) == keep_ref[...])
    spread = one_hot(quot(iota((slot_n, rows_in), 1), per_clip) == iota((slot_n, rows_in), 0))
    by_row = dot(named, spread).astype(BF16)
    wanted = one_hot(quot(iota((rows_out, enc_n), 0), per_clip) == train_ref[...])
    chosen = dot(wanted, by_row)
    row_at = rest(iota((rows_out, rows_in), 0), per_clip)
    col_at = rest(iota((rows_out, rows_in), 1), per_clip)
    same = (quot(row_at, chan) == rest(col_at, frame_n)) & (
        rest(row_at, chan) == quot(col_at, frame_n)
    )
    chosen = jnp.where(same, chosen, 0.0).astype(BF16)
    flat_frames = jnp.concatenate(
        [frames_ref[s, i].astype(F32) for s in range(slot_n) for i in range(chan)], axis=0
    ).astype(BF16)
    picked = dot(chosen, flat_frames).astype(BF16)
    packed[...] = picked.reshape(packed.shape)

    pl.semaphore_wait(barrier, peers - 1 + (clip_n - 1) * rows_near * times_near)

    def frame_copy(k, dt, dr):
        if dr == 0:
            src, dst = pl.ds(0, cells), pl.ds(halo_cells, cells)
        elif dr == 1:
            src, dst = pl.ds(cells - halo_cells, halo_cells), pl.ds(0, halo_cells)
        else:
            src, dst = pl.ds(0, halo_cells), pl.ds(halo_cells + cells, halo_cells)
        goal = lax.rem(c + k, clip_n)
        return pltpu.make_async_remote_copy(
            src_ref=packed.at[goal, :, src],
            dst_ref=landed.at[k, dt, :, dst],
            send_sem=frame_send.at[k, dt, dr + 1],
            recv_sem=frame_recv.at[k, dt, dr + 1],
            device_id={"clip": goal, "row": r + dr, "tm": t + dt},
            device_id_type=MESH,
        )

    moves = [
        (k, dt, dr)
        for k in range(clip_n - 1, -1, -1)
        for dt in (1, 0)
        for dr in (1, -1, 0)
        if (k, dt, dr) != (0, 0, 0)
    ]

    def each_move(sign, act):
        for k, dt, dr in moves:
            rr, tt = r + sign * dr, t + sign * dt
            if dr == 0 and dt == 0:
                act(frame_copy(k, dt, dr))
                continue

            @pl.when((rr >= 0) & (rr < row_dev) & (tt >= 0) & (tt < time_dev))
            def _():
                act(frame_copy(k, dt, dr))

    each_move(1, lambda copy: copy.start())
    landed[0, 0, :, halo_cells : halo_cells + cells] = packed[c]

    frames_wide = 2 * frame_n
    lines = frames_wide * chan
    depth = 256
    loads[3].wait()
    stem_w = stem_w_ref[...]
    taps_n = stem_w.shape[0]
    at = iota((depth, taps_n), 0)
    shift_at = quot(at, lines)
    in_shift = rest(at, lines)
    frame_at = quot(in_shift, chan)
    chan_at = in_shift - frame_at * chan
    tap_at = iota((depth, taps_n), 1)
    columns = []
    for f in range(ext_f):
        a = frame_at - f
        index = (a * (TAPS * TAPS) + shift_at) * chan + chan_at
        ok = (a >= 0) & (a < TAPS) & (at < TAPS * TAPS * lines) & (index == tap_at)
        columns.append(dot(one_hot(ok), stem_w).astype(BF16))
    stem_big = jnp.concatenate(columns, axis=1)

    lane = iota((128, 128), 1)
    source = iota((128, 128), 0)
    in_row = lane & (COLS - 1)
    col = 2 * (in_row & (COLS // 2 - 1)) + jnp.where(in_row >= COLS // 2, 1, 0)
    tables = []
    for tap in range(TAPS):
        moved = col + (tap - 1)
        ok = (moved >= 0) & (moved < COLS) & (source == (lane - in_row) + moved)
        tables.append(one_hot(ok))
    col_table = jnp.concatenate(tables, axis=1)

    half_rows = clips * per_clip
    total_rows = 2 * half_rows
    row_at = iota((total_rows, total_rows), 0)
    clip_at = quot(row_at, lines)
    in_clip = rest(row_at, lines)
    frame_at = quot(in_clip, chan)
    chan_at = in_clip - frame_at * chan
    base = clip_at * per_clip + chan_at
    before = jnp.where(t > 0, half_rows + base + frame_at * chan, base)
    goal = jnp.where(frame_at >= frame_n, base + (frame_at - frame_n) * chan, before)
    order = one_hot(goal == iota((total_rows, total_rows), 1))

    def group_table(chan_n):
        per_group = chan_n // GROUPS
        group_at = quot(iota((chan_n, chan_n), 0), per_group)
        return one_hot(group_at == quot(iota((chan_n, chan_n), 1), per_group))

    joined_mid, joined_out = group_table(chan_mid), group_table(chan_out)

    each_move(-1, lambda copy: copy.wait_recv())

    volume = landed[0].astype(F32)
    for k in range(1, clip_n):
        volume = volume + landed[k].astype(F32)
    volume = volume.astype(BF16).reshape(total_rows, wide)
    volume = dot(order, volume).astype(BF16)
    blocks = wide // 128
    stacked = jnp.concatenate(
        [volume[:, b * 128 : (b + 1) * 128] for b in range(blocks)], axis=0
    )
    shifted = dot(stacked, col_table)
    views = []
    by_tap = []
    for tap in range(TAPS):
        by_tap.append(
            jnp.concatenate(
                [
                    shifted[b * total_rows : (b + 1) * total_rows, tap * 128 : (tap + 1) * 128]
                    for b in range(blocks)
                ],
                axis=1,
            )
        )
    for row_tap in range(TAPS):
        for tap in range(TAPS):
            if row_tap % 2:
                views.append(
                    pltpu.roll(by_tap[tap], wide - row_tap * COLS, 1)[:, :out_cells]
                )
            else:
                views.append(by_tap[tap][:, row_tap * COLS : row_tap * COLS + out_cells])
    for number, view in enumerate(views):
        view_scr[number] = view
    filler = jnp.zeros((depth - TAPS * TAPS * lines, out_cells), F32)

    def sum_copy(number, j):
        other = lax.rem(me + j, peers)
        return pltpu.make_async_remote_copy(
            src_ref=sums[number].at[0],
            dst_ref=sums[number].at[j],
            send_sem=sum_send.at[number],
            recv_sem=sum_recv.at[number],
            device_id={"row": other // time_dev, "tm": lax.rem(other, time_dev)},
            device_id_type=MESH,
        )

    def sum_wait(number, semaphore):
        others = sums[number].at[pl.ds(1, peers - 1)]
        pltpu.make_async_copy(others, others, semaphore.at[number]).wait()

    def send_sums(number, own, group):
        for place, k in enumerate(group):
            low = len(group) + place
            sums[number][0, place : place + 1, :] = own[k, 0:1, :]
            sums[number][0, low : low + 1, :] = own[k, 1:2, :]

        @pl.loop(1, peers)
        def _(j):
            sum_copy(number, j).start()

    def take_sums(number, joined, gain, shift, norm, group):
        sum_wait(number, sum_recv)
        total = sums[number][0]
        for j in range(1, peers):
            total = total + sums[number][j]
        rows = total.shape[0]
        high = total.astype(BF16).astype(F32)
        middle = (total - high).astype(BF16).astype(F32)
        low = total - high - middle
        joint = dot(jnp.concatenate([high, middle, low], axis=0).astype(BF16), joined)
        total = joint[:rows] + joint[rows : 2 * rows] + joint[2 * rows :]
        per_group = total.shape[1] // GROUPS
        total = total * (1.0 / (peers * frame_n * cells * per_group))
        mean = total[: rows // 2]
        inverse = lax.rsqrt(total[rows // 2 :] - mean * mean + eps)
        scale = inverse * gain
        move = shift - mean * scale
        for place, k in enumerate(group):
            norm[k, 0:1, :] = scale[place : place + 1]
            norm[k, 1:2, :] = move[place : place + 1]

    @pl.loop(0, clips)
    def _(k):
        first_line = pl.multiple_of(k * lines, 8)
        patches = jnp.concatenate(
            [view_scr[number, pl.ds(first_line, lines), :] for number in range(TAPS * TAPS)]
            + [filler],
            axis=0,
        ).astype(BF16)
        stem = lax.dot_general(
            patches, stem_big, (((0,), (0,)), ((), ())), preferred_element_type=F32
        )
        value_sum = jnp.zeros((1, chan_mid), F32)
        square_sum = jnp.zeros((1, chan_mid), F32)
        for f in range(ext_f):
            part = stem[:, f * chan_mid : (f + 1) * chan_mid]
            stem_scr[k, f] = part
            if f >= HALO:
                own = part[COLS : COLS + cells]
                value_sum = value_sum + jnp.sum(own, axis=0, keepdims=True)
                square_sum = square_sum + jnp.sum(own * own, axis=0, keepdims=True)
        own1[k, 0:1, :] = value_sum
        own1[k, 1:2, :] = square_sum
        for number, group in enumerate(rounds1):

            @pl.when(k == group[-1])
            def _():
                send_sums(number, own1, group)

    top = jnp.where(r > 0, 1.0, 0.0).astype(F32)
    bottom = jnp.where(r < row_dev - 1, 1.0, 0.0).astype(F32)
    ext_rows = row_n + 2
    half_cols = COLS // 2
    x_at = iota((ext_rows * half_cols, chan_mid), 0) & (half_cols - 1)

    def norm_first(k, frames_at):
        scale, shift = norm1[k, 0:1, :], norm1[k, 1:2, :]
        for f in frames_at:
            value = stem_scr[k, f]
            value = silu(value * scale + shift)
            value = jnp.concatenate(
                [
                    value[:COLS] * top,
                    value[COLS : COLS + cells],
                    value[COLS + cells :] * bottom,
                ],
                axis=0,
            )
            parts = value.reshape(ext_rows, 2, half_cols, chan_mid)
            even, odd = parts[:, 0], parts[:, 1]
            flat = (ext_rows * half_cols, chan_mid)
            left = jnp.where(x_at == 0, 0.0, pltpu.roll(odd.reshape(flat), 1, 0))
            right = jnp.where(
                x_at == half_cols - 1, 0.0, pltpu.roll(even.reshape(flat), flat[0] - 1, 0)
            )
            left = left.reshape(even.shape)
            right = right.reshape(even.shape)
            before = jnp.stack([left, even], axis=1).reshape(value.shape)
            after = jnp.stack([odd, right], axis=1).reshape(value.shape)
            hidden_scr[k, f, :, :chan_mid] = before.astype(BF16)
            hidden_scr[k, f, :, chan_mid : 2 * chan_mid] = value.astype(BF16)
            hidden_scr[k, f, :, 2 * chan_mid :] = after.astype(BF16)

    def mix(k, first, count):
        strip = jnp.concatenate(
            [
                hidden_scr[
                    k, pl.ds(first + a, count), b * COLS : b * COLS + cells, :
                ].reshape(count * cells, TAPS * chan_mid)
                for a in range(TAPS)
                for b in range(TAPS)
            ],
            axis=1,
        )
        mixed = dot(strip, mixer_w[...])
        mixer_scr[k, pl.ds(first, count)] = mixed.reshape(count, cells, chan_out)
        return (
            jnp.sum(mixed, axis=0, keepdims=True),
            jnp.sum(mixed * mixed, axis=0, keepdims=True),
        )

    for load in loads[4:7]:
        load.wait()
    step = frame_n // 2

    @pl.loop(0, clips)
    def _(k):
        for number, group in enumerate(rounds1):

            @pl.when(k == group[0])
            def _():
                take_sums(
                    number, joined_mid, stem_gain_ref[...], stem_shift_ref[...], norm1, group
                )

        @pl.loop(0, ext_f // 2)
        def _(f):
            norm_first(k, (2 * f, 2 * f + 1))

        def mix_step(i, so_far):
            value_sum, square_sum = mix(k, i * step, step)
            return so_far[0] + value_sum, so_far[1] + square_sum

        nothing = jnp.zeros((1, chan_out), F32)
        value_sum, square_sum = lax.fori_loop(0, frame_n // step, mix_step, (nothing, nothing))
        own2[k, 0:1, :] = value_sum
        own2[k, 1:2, :] = square_sum
        for number, group in enumerate(rounds2):

            @pl.when(k == group[-1])
            def _():
                send_sums(len(rounds1) + number, own2, group)

    for load in loads[7:]:
        load.wait()
    bias = down_bias_ref[...]
    pairs = frame_n // 2
    out_rows = row_n // 2
    size = pairs * out_rows * half_cols

    @pl.loop(0, clips)
    def _(k):
        for number, group in enumerate(rounds2):

            @pl.when(k == group[0])
            def _():
                take_sums(
                    len(rounds1) + number,
                    joined_out,
                    mixer_gain_ref[...],
                    mixer_shift_ref[...],
                    norm2,
                    group,
                )

        scale, shift = norm2[k, 0:1, :], norm2[k, 1:2, :]
        squares = []
        for pair in range(pairs):
            acts = []
            for f in (2 * pair, 2 * pair + 1):
                value = mixer_scr[k, f] * scale + shift
                acts.append(silu(value).astype(BF16).astype(F32))
            pooled = ((acts[0] + acts[1]) * 0.5).astype(BF16)
            pooled = pooled.reshape(out_rows, 2, 2, half_cols, chan_out)
            squares.append(
                jnp.concatenate(
                    [
                        pooled[:, p, q].reshape(out_rows * half_cols, chan_out)
                        for p in range(2)
                        for q in range(2)
                    ],
                    axis=1,
                )
            )
        block = jnp.concatenate(squares, axis=0)
        latent = dot(block, down_w[...]) + bias
        out_ref[pl.ds(pl.multiple_of(k * size, size), size), :] = latent.astype(BF16)

    each_move(1, lambda copy: copy.wait_send())
    for number in range(len(sums)):
        sum_wait(number, sum_send)


def local(
    frames,
    keep_list,
    train_slot,
    stem_weight,
    stem_gain,
    stem_shift,
    mixer_weight,
    mixer_gain,
    mixer_shift,
    down_weight,
    down_bias,
):
    clip_n = lax.axis_size("clip")
    row_dev = lax.axis_size("row")
    time_dev = lax.axis_size("tm")
    slots, chan, frame_n, cells = frames.shape
    clips = train_slot.shape[0] // clip_n
    row_n = cells // COLS
    chan_mid = stem_weight.shape[1]
    chan_out = mixer_weight.shape[3]
    every = tuple(range(clips))
    rounds1 = tuple(part for part in (every[:1], every[1:]) if part)
    rounds2 = tuple(part for part in (every[:-1], every[-1:]) if part)
    peers = row_dev * time_dev
    ext_f = frame_n + HALO
    out_cells = cells + 2 * COLS
    sizes = (clip_n, row_dev, time_dev, clips, chan, frame_n, row_n, rounds1, rounds2)
    out_rows = clips * (frame_n // 2) * (row_n // 2) * (COLS // 2)
    operands = (
        frames,
        keep_list[None],
        train_slot[None],
        stem_weight,
        stem_gain[None],
        stem_shift[None],
        mixer_weight.reshape(-1, chan_out),
        mixer_gain[None],
        mixer_shift[None],
        down_weight,
        down_bias[None],
    )
    vmem = pl.BlockSpec(memory_space=pltpu.VMEM)
    hbm = pl.BlockSpec(memory_space=pltpu.HBM)
    out = pl.pallas_call(
        functools.partial(kernel, sizes),
        out_shape=jax.ShapeDtypeStruct((out_rows, chan_out), BF16),
        in_specs=[hbm] * len(operands),
        out_specs=vmem,
        scratch_shapes=[pltpu.VMEM(operand.shape, operand.dtype) for operand in operands]
        + [
            pltpu.VMEM((clip_n, clips * frame_n * chan, cells), BF16),
            pltpu.VMEM((clip_n, 2, clips * frame_n * chan, cells + 2 * HALO * COLS), BF16),
            pltpu.VMEM((clips, ext_f, out_cells, chan_mid), F32),
            pltpu.VMEM((clips, ext_f, out_cells, TAPS * chan_mid), BF16),
            pltpu.VMEM((clips, frame_n, cells, chan_out), F32),
            pltpu.VMEM((TAPS * TAPS, 2 * clips * frame_n * chan, out_cells), F32),
            pltpu.VMEM((clips, 2, chan_mid), F32),
            pltpu.VMEM((clips, 2, chan_out), F32),
            pltpu.VMEM((clips, 2, chan_mid), F32),
            pltpu.VMEM((clips, 2, chan_out), F32),
            pltpu.SemaphoreType.DMA((len(operands),)),
            pltpu.SemaphoreType.DMA((clip_n, 2, 3)),
            pltpu.SemaphoreType.DMA((clip_n, 2, 3)),
            pltpu.SemaphoreType.DMA((len(rounds1) + len(rounds2),)),
            pltpu.SemaphoreType.DMA((len(rounds1) + len(rounds2),)),
        ]
        + [pltpu.VMEM((peers, 2 * len(part), chan_mid), F32) for part in rounds1]
        + [pltpu.VMEM((peers, 2 * len(part), chan_out), F32) for part in rounds2],
        compiler_params=pltpu.CompilerParams(
            collective_id=0, has_side_effects=True, vmem_limit_bytes=64 * 1024 * 1024
        ),
    )(*operands)
    return out.reshape(clips, frame_n // 2, row_n // 2, COLS // 2, chan_out)


def solution(mesh):
    return jax.shard_map(
        local,
        mesh=mesh,
        in_specs=(
            P("clip", None, "tm", "row"),
            P("clip"),
            P(),
            P(),
            P(),
            P(),
            P(),
            P(),
            P(),
            P(),
            P(),
        ),
        out_specs=P("clip", "tm", "row", None, None),
        check_vma=False,
    )
```

```python
import functools

import jax
import jax.numpy as jnp
from jax import lax
from jax.experimental import pallas as pl
from jax.experimental.pallas import tpu as pltpu
from jax.sharding import PartitionSpec as P

GROUPS = 32
COLS = 64
HALO = 2
TAPS = 3
MESH = pl.DeviceIdType.MESH
F32 = jnp.float32
BF16 = jnp.bfloat16

eps = 1e-06


def iota(shape, dim):
    return lax.broadcasted_iota(jnp.int32, shape, dim)


def quot(value, by):
    return lax.shift_right_logical(value * (65536 // by + 1), 16)


def rest(value, by):
    return value - quot(value, by) * by


def dot(left, right):
    return jnp.dot(left, right, preferred_element_type=F32)


def silu(value):
    half = value * 0.5
    return half + half * jnp.tanh(half)


def one_hot(flag):
    return jnp.where(flag, 1.0, 0.0).astype(BF16)


def kernel(
    sizes,
    frames_hbm,
    keep_hbm,
    train_hbm,
    stem_w_hbm,
    stem_gain_hbm,
    stem_shift_hbm,
    mixer_w_hbm,
    mixer_gain_hbm,
    mixer_shift_hbm,
    down_w_hbm,
    down_bias_hbm,
    out_ref,
    frames_ref,
    keep_ref,
    train_ref,
    stem_w_ref,
    stem_gain_ref,
    stem_shift_ref,
    mixer_w,
    mixer_gain_ref,
    mixer_shift_ref,
    down_w,
    down_bias_ref,
    packed,
    landed,
    stem_scr,
    hidden_scr,
    mixer_scr,
    load_sem,
    frame_send,
    frame_recv,
    sum_send,
    sum_recv,
    *sums,
):
    clip_n, row_dev, time_dev, clips, chan, frame_n, row_n, rounds1, rounds2 = sizes
    cells = row_n * COLS
    c = lax.axis_index("clip")
    r = lax.axis_index("row")
    t = lax.axis_index("tm")
    me = r * time_dev + t
    peers = row_dev * time_dev
    per_clip = frame_n * chan
    halo_cells = HALO * COLS
    wide = cells + 2 * halo_cells
    out_cells = cells + 2 * COLS
    ext_f = frame_n + HALO
    chan_mid = stem_w_ref.shape[1]
    chan_out = mixer_w.shape[1]

    loads = [
        pltpu.make_async_copy(source, target, load_sem.at[number])
        for number, (source, target) in enumerate(
            (
                (frames_hbm, frames_ref),
                (keep_hbm, keep_ref),
                (train_hbm, train_ref),
                (stem_w_hbm, stem_w_ref),
                (stem_gain_hbm, stem_gain_ref),
                (stem_shift_hbm, stem_shift_ref),
                (mixer_w_hbm, mixer_w),
                (mixer_gain_hbm, mixer_gain_ref),
                (mixer_shift_hbm, mixer_shift_ref),
                (down_w_hbm, down_w),
                (down_bias_hbm, down_bias_ref),
            )
        )
    ]
    for load in loads:
        load.start()

    landed[...] = jnp.zeros_like(landed)

    barrier = pltpu.get_barrier_semaphore()
    for j in range(1, peers):
        other = lax.rem(me + j, peers)
        pl.semaphore_signal(
            barrier,
            inc=1,
            device_id={"row": other // time_dev, "tm": lax.rem(other, time_dev)},
            device_id_type=MESH,
        )
    rows_near = 1 + (r > 0).astype(jnp.int32) + (r < row_dev - 1).astype(jnp.int32)
    times_near = 1 + (t > 0).astype(jnp.int32) + (t < time_dev - 1).astype(jnp.int32)
    for k in range(1, clip_n):
        for dr in (-1, 0, 1):
            for dt in (-1, 0, 1):

                @pl.when((r + dr >= 0) & (r + dr < row_dev) & (t + dt >= 0) & (t + dt < time_dev))
                def _():
                    pl.semaphore_signal(
                        barrier,
                        inc=1,
                        device_id={"clip": lax.rem(c + k, clip_n), "row": r + dr, "tm": t + dt},
                        device_id_type=MESH,
                    )

    for load in loads[:3]:
        load.wait()

    slot_n = keep_ref.shape[1]
    enc_n = train_ref.shape[1]
    rows_in = slot_n * per_clip
    rows_out = enc_n * per_clip
    named = one_hot(iota((enc_n, slot_n), 0) == keep_ref[...])
    spread = one_hot(quot(iota((slot_n, rows_in), 1), per_clip) == iota((slot_n, rows_in), 0))
    by_row = dot(named, spread).astype(BF16)
    wanted = one_hot(quot(iota((rows_out, enc_n), 0), per_clip) == train_ref[...])
    chosen = dot(wanted, by_row)
    row_at = rest(iota((rows_out, rows_in), 0), per_clip)
    col_at = rest(iota((rows_out, rows_in), 1), per_clip)
    same = (quot(row_at, chan) == rest(col_at, frame_n)) & (
        rest(row_at, chan) == quot(col_at, frame_n)
    )
    chosen = jnp.where(same, chosen, 0.0).astype(BF16)
    flat_frames = jnp.concatenate(
        [frames_ref[s, i].astype(F32) for s in range(slot_n) for i in range(chan)], axis=0
    ).astype(BF16)
    picked = dot(chosen, flat_frames).astype(BF16)
    packed[...] = picked.reshape(packed.shape)

    pl.semaphore_wait(barrier, peers - 1 + (clip_n - 1) * rows_near * times_near)

    def frame_copy(k, dt, dr):
        if dr == 0:
            src, dst = pl.ds(0, cells), pl.ds(halo_cells, cells)
        elif dr == 1:
            src, dst = pl.ds(cells - halo_cells, halo_cells), pl.ds(0, halo_cells)
        else:
            src, dst = pl.ds(0, halo_cells), pl.ds(halo_cells + cells, halo_cells)
        goal = lax.rem(c + k, clip_n)
        return pltpu.make_async_remote_copy(
            src_ref=packed.at[goal, :, src],
            dst_ref=landed.at[k, dt, :, dst],
            send_sem=frame_send.at[k, dt, dr + 1],
            recv_sem=frame_recv.at[k, dt, dr + 1],
            device_id={"clip": goal, "row": r + dr, "tm": t + dt},
            device_id_type=MESH,
        )

    moves = [
        (k, dt, dr)
        for k in range(clip_n - 1, -1, -1)
        for dt in (1, 0)
        for dr in (1, -1, 0)
        if (k, dt, dr) != (0, 0, 0)
    ]

    def each_move(sign, act):
        for k, dt, dr in moves:
            rr, tt = r + sign * dr, t + sign * dt
            if dr == 0 and dt == 0:
                act(frame_copy(k, dt, dr))
                continue

            @pl.when((rr >= 0) & (rr < row_dev) & (tt >= 0) & (tt < time_dev))
            def _():
                act(frame_copy(k, dt, dr))

    each_move(1, lambda copy: copy.start())
    landed[0, 0, :, halo_cells : halo_cells + cells] = packed[c]

    frames_wide = 2 * frame_n
    lines = frames_wide * chan
    depth = 256
    loads[3].wait()
    stem_w = stem_w_ref[...]
    taps_n = stem_w.shape[0]
    at = iota((depth, taps_n), 0)
    shift_at = quot(at, lines)
    in_shift = rest(at, lines)
    frame_at = quot(in_shift, chan)
    chan_at = in_shift - frame_at * chan
    tap_at = iota((depth, taps_n), 1)
    columns = []
    for f in range(ext_f):
        a = frame_at - f
        index = (a * (TAPS * TAPS) + shift_at) * chan + chan_at
        ok = (a >= 0) & (a < TAPS) & (at < TAPS * TAPS * lines) & (index == tap_at)
        columns.append(dot(one_hot(ok), stem_w).astype(BF16))
    stem_big = jnp.concatenate(columns, axis=1)

    lane = iota((128, 128), 1)
    source = iota((128, 128), 0)
    in_row = lane & (COLS - 1)
    col = 2 * (in_row & (COLS // 2 - 1)) + jnp.where(in_row >= COLS // 2, 1, 0)
    tables = []
    for tap in range(TAPS):
        moved = col + (tap - 1)
        ok = (moved >= 0) & (moved < COLS) & (source == (lane - in_row) + moved)
        tables.append(one_hot(ok))
    col_table = jnp.concatenate(tables, axis=1)

    half_rows = clips * per_clip
    total_rows = 2 * half_rows
    row_at = iota((total_rows, total_rows), 0)
    clip_at = quot(row_at, lines)
    in_clip = rest(row_at, lines)
    frame_at = quot(in_clip, chan)
    chan_at = in_clip - frame_at * chan
    base = clip_at * per_clip + chan_at
    before = jnp.where(t > 0, half_rows + base + frame_at * chan, base)
    goal = jnp.where(frame_at >= frame_n, base + (frame_at - frame_n) * chan, before)
    order = one_hot(goal == iota((total_rows, total_rows), 1))

    def group_table(chan_n):
        per_group = chan_n // GROUPS
        group_at = quot(iota((chan_n, chan_n), 0), per_group)
        return one_hot(group_at == quot(iota((chan_n, chan_n), 1), per_group))

    joined_mid, joined_out = group_table(chan_mid), group_table(chan_out)

    each_move(-1, lambda copy: copy.wait_recv())

    volume = landed[0].astype(F32)
    for k in range(1, clip_n):
        volume = volume + landed[k].astype(F32)
    volume = volume.astype(BF16).reshape(total_rows, wide)
    volume = dot(order, volume).astype(BF16)
    blocks = wide // 128
    stacked = jnp.concatenate(
        [volume[:, b * 128 : (b + 1) * 128] for b in range(blocks)], axis=0
    )
    shifted = dot(stacked, col_table)
    views = []
    by_tap = []
    for tap in range(TAPS):
        by_tap.append(
            jnp.concatenate(
                [
                    shifted[b * total_rows : (b + 1) * total_rows, tap * 128 : (tap + 1) * 128]
                    for b in range(blocks)
                ],
                axis=1,
            )
        )
    for row_tap in range(TAPS):
        for tap in range(TAPS):
            if row_tap % 2:
                views.append(
                    pltpu.roll(by_tap[tap], wide - row_tap * COLS, 1)[:, :out_cells]
                )
            else:
                views.append(by_tap[tap][:, row_tap * COLS : row_tap * COLS + out_cells])
    filler = jnp.zeros((depth - TAPS * TAPS * lines, out_cells), F32)

    def sum_copy(number, j):
        other = lax.rem(me + j, peers)
        return pltpu.make_async_remote_copy(
            src_ref=sums[number].at[0],
            dst_ref=sums[number].at[j],
            send_sem=sum_send.at[number],
            recv_sem=sum_recv.at[number],
            device_id={"row": other // time_dev, "tm": lax.rem(other, time_dev)},
            device_id_type=MESH,
        )

    def sum_wait(number, semaphore):
        others = sums[number].at[pl.ds(1, peers - 1)]
        pltpu.make_async_copy(others, others, semaphore.at[number]).wait()

    def send_sums(number, clip_sums):
        for place, (value_sum, square_sum) in enumerate(clip_sums):
            low = len(clip_sums) + place
            sums[number][0, place : place + 1, :] = value_sum
            sums[number][0, low : low + 1, :] = square_sum
        for j in range(1, peers):
            sum_copy(number, j).start()

    def take_sums(number, joined, gain, shift):
        sum_wait(number, sum_recv)
        total = sums[number][0]
        for j in range(1, peers):
            total = total + sums[number][j]
        rows = total.shape[0]
        high = total.astype(BF16).astype(F32)
        middle = (total - high).astype(BF16).astype(F32)
        low = total - high - middle
        joint = dot(jnp.concatenate([high, middle, low], axis=0).astype(BF16), joined)
        total = joint[:rows] + joint[rows : 2 * rows] + joint[2 * rows :]
        per_group = total.shape[1] // GROUPS
        total = total * (1.0 / (peers * frame_n * cells * per_group))
        mean = total[: rows // 2]
        inverse = lax.rsqrt(total[rows // 2 :] - mean * mean + eps)
        scale = inverse * gain
        move = shift - mean * scale
        return [(scale[i : i + 1], move[i : i + 1]) for i in range(rows // 2)]

    for number, group in enumerate(rounds1):
        clip_sums = []
        for k in group:
            patches = jnp.concatenate(
                [view[k * lines : (k + 1) * lines] for view in views] + [filler], axis=0
            ).astype(BF16)
            stem = lax.dot_general(
                patches, stem_big, (((0,), (0,)), ((), ())), preferred_element_type=F32
            )
            stem_scr[k] = stem
            own = stem[COLS : COLS + cells, HALO * chan_mid :]
            values = jnp.sum(own, axis=0, keepdims=True)
            squares = jnp.sum(own * own, axis=0, keepdims=True)
            value_sum = values[:, :chan_mid]
            square_sum = squares[:, :chan_mid]
            for f in range(1, frame_n):
                value_sum = value_sum + values[:, f * chan_mid : (f + 1) * chan_mid]
                square_sum = square_sum + squares[:, f * chan_mid : (f + 1) * chan_mid]
            clip_sums.append((value_sum, square_sum))
        send_sums(number, clip_sums)

    top = jnp.where(r > 0, 1.0, 0.0).astype(F32)
    bottom = jnp.where(r < row_dev - 1, 1.0, 0.0).astype(F32)
    ext_rows = row_n + 2
    half_cols = COLS // 2
    x_at = iota((ext_rows * half_cols, chan_mid), 0) & (half_cols - 1)

    def norm_first(k, frames_at, scale, shift):
        for f in frames_at:
            value = stem_scr[k, :, f * chan_mid : (f + 1) * chan_mid]
            value = silu(value * scale + shift)
            value = jnp.concatenate(
                [
                    value[:COLS] * top,
                    value[COLS : COLS + cells],
                    value[COLS + cells :] * bottom,
                ],
                axis=0,
            )
            parts = value.reshape(ext_rows, 2, half_cols, chan_mid)
            even, odd = parts[:, 0], parts[:, 1]
            flat = (ext_rows * half_cols, chan_mid)
            left = jnp.where(x_at == 0, 0.0, pltpu.roll(odd.reshape(flat), 1, 0))
            right = jnp.where(
                x_at == half_cols - 1, 0.0, pltpu.roll(even.reshape(flat), flat[0] - 1, 0)
            )
            left = left.reshape(even.shape)
            right = right.reshape(even.shape)
            before = jnp.stack([left, even], axis=1).reshape(value.shape)
            after = jnp.stack([odd, right], axis=1).reshape(value.shape)
            hidden_scr[k, f, :, :chan_mid] = before.astype(BF16)
            hidden_scr[k, f, :, chan_mid : 2 * chan_mid] = value.astype(BF16)
            hidden_scr[k, f, :, 2 * chan_mid :] = after.astype(BF16)

    def mix(k, first, count):
        strip = jnp.concatenate(
            [
                hidden_scr[k, first + a : first + a + count, b * COLS : b * COLS + cells, :].reshape(
                    count * cells, TAPS * chan_mid
                )
                for a in range(TAPS)
                for b in range(TAPS)
            ],
            axis=1,
        )
        mixed = dot(strip, mixer_w[...])
        mixer_scr[k, first : first + count] = mixed.reshape(count, cells, chan_out)
        return (
            jnp.sum(mixed, axis=0, keepdims=True),
            jnp.sum(mixed * mixed, axis=0, keepdims=True),
        )

    for load in loads[4:7]:
        load.wait()
    norms = {}

    def take_first(number):
        taken = take_sums(number, joined_mid, stem_gain_ref[...], stem_shift_ref[...])
        norms.update(zip(rounds1[number], taken))

    take_first(0)
    norm_first(0, range(ext_f), *norms[0])
    half = frame_n // 2
    done = []
    for k in range(clips):
        low_sums = mix(k, 0, half)
        if k + 1 < clips:
            if k + 1 not in norms:
                take_first(1)
            norm_first(k + 1, range(ext_f), *norms[k + 1])
        high_sums = mix(k, half, frame_n - half)
        done.append((low_sums[0] + high_sums[0], low_sums[1] + high_sums[1]))
        for number, group in enumerate(rounds2):
            if group[-1] == k:
                send_sums(len(rounds1) + number, [done[i] for i in group])

    for load in loads[7:]:
        load.wait()
    bias = down_bias_ref[...]
    pairs = frame_n // 2
    out_rows = row_n // 2
    for number, group in enumerate(rounds2):
        taken = take_sums(
            len(rounds1) + number, joined_out, mixer_gain_ref[...], mixer_shift_ref[...]
        )
        for k, (scale, shift) in zip(group, taken):
            squares = []
            for pair in range(pairs):
                acts = []
                for f in (2 * pair, 2 * pair + 1):
                    value = mixer_scr[k, f] * scale + shift
                    acts.append(silu(value).astype(BF16).astype(F32))
                pooled = ((acts[0] + acts[1]) * 0.5).astype(BF16)
                pooled = pooled.reshape(out_rows, 2, 2, half_cols, chan_out)
                squares.append(
                    jnp.concatenate(
                        [
                            pooled[:, p, q].reshape(out_rows * half_cols, chan_out)
                            for p in range(2)
                            for q in range(2)
                        ],
                        axis=1,
                    )
                )
            block = jnp.concatenate(squares, axis=0)
            latent = dot(block, down_w[...]) + bias
            size = block.shape[0]
            out_ref[k * size : (k + 1) * size, :] = latent.astype(BF16)

    each_move(1, lambda copy: copy.wait_send())
    for number in range(len(sums)):
        sum_wait(number, sum_send)


def local(
    frames,
    keep_list,
    train_slot,
    stem_weight,
    stem_gain,
    stem_shift,
    mixer_weight,
    mixer_gain,
    mixer_shift,
    down_weight,
    down_bias,
):
    clip_n = lax.axis_size("clip")
    row_dev = lax.axis_size("row")
    time_dev = lax.axis_size("tm")
    slots, chan, frame_n, cells = frames.shape
    clips = train_slot.shape[0] // clip_n
    row_n = cells // COLS
    chan_mid = stem_weight.shape[1]
    chan_out = mixer_weight.shape[3]
    every = tuple(range(clips))
    rounds1 = tuple(part for part in (every[:1], every[1:]) if part)
    rounds2 = tuple(part for part in (every[:-1], every[-1:]) if part)
    peers = row_dev * time_dev
    ext_f = frame_n + HALO
    out_cells = cells + 2 * COLS
    sizes = (clip_n, row_dev, time_dev, clips, chan, frame_n, row_n, rounds1, rounds2)
    out_rows = clips * (frame_n // 2) * (row_n // 2) * (COLS // 2)
    operands = (
        frames,
        keep_list[None],
        train_slot[None],
        stem_weight,
        stem_gain[None],
        stem_shift[None],
        mixer_weight.reshape(-1, chan_out),
        mixer_gain[None],
        mixer_shift[None],
        down_weight,
        down_bias[None],
    )
    vmem = pl.BlockSpec(memory_space=pltpu.VMEM)
    hbm = pl.BlockSpec(memory_space=pltpu.HBM)
    out = pl.pallas_call(
        functools.partial(kernel, sizes),
        out_shape=jax.ShapeDtypeStruct((out_rows, chan_out), BF16),
        in_specs=[hbm] * len(operands),
        out_specs=vmem,
        scratch_shapes=[pltpu.VMEM(operand.shape, operand.dtype) for operand in operands]
        + [
            pltpu.VMEM((clip_n, clips * frame_n * chan, cells), BF16),
            pltpu.VMEM((clip_n, 2, clips * frame_n * chan, cells + 2 * HALO * COLS), BF16),
            pltpu.VMEM((clips, out_cells, ext_f * chan_mid), F32),
            pltpu.VMEM((clips, ext_f, out_cells, TAPS * chan_mid), BF16),
            pltpu.VMEM((clips, frame_n, cells, chan_out), F32),
            pltpu.SemaphoreType.DMA((len(operands),)),
            pltpu.SemaphoreType.DMA((clip_n, 2, 3)),
            pltpu.SemaphoreType.DMA((clip_n, 2, 3)),
            pltpu.SemaphoreType.DMA((len(rounds1) + len(rounds2),)),
            pltpu.SemaphoreType.DMA((len(rounds1) + len(rounds2),)),
        ]
        + [pltpu.VMEM((peers, 2 * len(part), chan_mid), F32) for part in rounds1]
        + [pltpu.VMEM((peers, 2 * len(part), chan_out), F32) for part in rounds2],
        compiler_params=pltpu.CompilerParams(
            collective_id=0, has_side_effects=True, vmem_limit_bytes=50 * 1024 * 1024
        ),
    )(*(pltpu.with_memory_space_constraint(operand, pltpu.HBM) for operand in operands))
    return out.reshape(clips, frame_n // 2, row_n // 2, COLS // 2, chan_out)


def solution(mesh):
    return jax.shard_map(
        local,
        mesh=mesh,
        in_specs=(
            P("clip", None, "tm", "row"),
            P("clip"),
            P(),
            P(),
            P(),
            P(),
            P(),
            P(),
            P(),
            P(),
            P(),
        ),
        out_specs=P("clip", "tm", "row", None, None),
        check_vma=False,
    )
```

```python
import functools

import jax
import jax.numpy as jnp
from jax import lax
from jax.experimental import pallas as pl
from jax.experimental.pallas import tpu as pltpu
from jax.sharding import PartitionSpec as P

GROUPS = 32
COLS = 64
HALO = 2
TAPS = 3
MESH = pl.DeviceIdType.MESH
F32 = jnp.float32
BF16 = jnp.bfloat16

eps = 1e-06


def iota(shape, dim):
    return lax.broadcasted_iota(jnp.int32, shape, dim)


def quot(value, by):
    return lax.shift_right_logical(value * (65536 // by + 1), 16)


def rest(value, by):
    return value - quot(value, by) * by


def dot(left, right):
    return jnp.dot(left, right, preferred_element_type=F32)


def silu(value):
    half = value * 0.5
    return half + half * jnp.tanh(half)


def one_hot(flag):
    return jnp.where(flag, 1.0, 0.0).astype(BF16)


def kernel(
    sizes,
    frames_hbm,
    keep_hbm,
    train_hbm,
    stem_w_hbm,
    stem_gain_hbm,
    stem_shift_hbm,
    mixer_w_hbm,
    mixer_gain_hbm,
    mixer_shift_hbm,
    down_w_hbm,
    down_bias_hbm,
    out_ref,
    frames_ref,
    keep_ref,
    train_ref,
    stem_w_ref,
    stem_gain_ref,
    stem_shift_ref,
    mixer_w,
    mixer_gain_ref,
    mixer_shift_ref,
    down_w,
    down_bias_ref,
    packed,
    landed,
    stem_scr,
    hidden_scr,
    mixer_scr,
    load_sem,
    frame_send,
    frame_recv,
    sum_send,
    sum_recv,
    *sums,
):
    clip_n, row_dev, time_dev, clips, chan, frame_n, row_n, rounds1, rounds2 = sizes
    cells = row_n * COLS
    c = lax.axis_index("clip")
    r = lax.axis_index("row")
    t = lax.axis_index("tm")
    rows_at = [jnp.where(r + j < row_dev, r + j, r + j - row_dev) for j in range(row_dev)]
    times_at = [jnp.where(t + j < time_dev, t + j, t + j - time_dev) for j in range(time_dev)]
    peers = row_dev * time_dev
    per_clip = frame_n * chan
    halo_cells = HALO * COLS
    wide = cells + 2 * halo_cells
    out_cells = cells + 2 * COLS
    ext_f = frame_n + HALO
    chan_mid = stem_w_ref.shape[1]
    chan_out = mixer_w.shape[1]

    loads = [
        pltpu.make_async_copy(source, target, load_sem.at[number])
        for number, (source, target) in enumerate(
            (
                (frames_hbm, frames_ref),
                (keep_hbm, keep_ref),
                (train_hbm, train_ref),
                (stem_w_hbm, stem_w_ref),
                (stem_gain_hbm, stem_gain_ref),
                (stem_shift_hbm, stem_shift_ref),
                (mixer_w_hbm, mixer_w),
                (mixer_gain_hbm, mixer_gain_ref),
                (mixer_shift_hbm, mixer_shift_ref),
                (down_w_hbm, down_w),
                (down_bias_hbm, down_bias_ref),
            )
        )
    ]
    for load in loads:
        load.start()

    landed[...] = jnp.zeros_like(landed)

    barrier = pltpu.get_barrier_semaphore()
    for j in range(1, peers):
        pl.semaphore_signal(
            barrier,
            inc=1,
            device_id={"row": rows_at[j // time_dev], "tm": times_at[j % time_dev]},
            device_id_type=MESH,
        )
    rows_near = 1 + (r > 0).astype(jnp.int32) + (r < row_dev - 1).astype(jnp.int32)
    times_near = 1 + (t > 0).astype(jnp.int32) + (t < time_dev - 1).astype(jnp.int32)
    for k in range(1, clip_n):
        for dr in (-1, 0, 1):
            for dt in (-1, 0, 1):

                @pl.when((r + dr >= 0) & (r + dr < row_dev) & (t + dt >= 0) & (t + dt < time_dev))
                def _():
                    pl.semaphore_signal(
                        barrier,
                        inc=1,
                        device_id={"clip": lax.rem(c + k, clip_n), "row": r + dr, "tm": t + dt},
                        device_id_type=MESH,
                    )

    for load in loads[:3]:
        load.wait()

    slot_n = keep_ref.shape[1]
    enc_n = train_ref.shape[1]
    rows_in = slot_n * per_clip
    rows_out = enc_n * per_clip
    named = one_hot(iota((enc_n, slot_n), 0) == keep_ref[...])
    spread = one_hot(quot(iota((slot_n, rows_in), 1), per_clip) == iota((slot_n, rows_in), 0))
    by_row = dot(named, spread).astype(BF16)
    wanted = one_hot(quot(iota((rows_out, enc_n), 0), per_clip) == train_ref[...])
    chosen = dot(wanted, by_row)
    row_at = rest(iota((rows_out, rows_in), 0), per_clip)
    col_at = rest(iota((rows_out, rows_in), 1), per_clip)
    same = (quot(row_at, chan) == rest(col_at, frame_n)) & (
        rest(row_at, chan) == quot(col_at, frame_n)
    )
    chosen = jnp.where(same, chosen, 0.0).astype(BF16)
    flat_frames = jnp.concatenate(
        [frames_ref[s, i].astype(F32) for s in range(slot_n) for i in range(chan)], axis=0
    ).astype(BF16)
    picked = dot(chosen, flat_frames).astype(BF16)
    packed[...] = picked.reshape(packed.shape)

    pl.semaphore_wait(barrier, peers - 1 + (clip_n - 1) * rows_near * times_near)

    def frame_copy(k, dt, dr):
        if dr == 0:
            src, dst = pl.ds(0, cells), pl.ds(halo_cells, cells)
        elif dr == 1:
            src, dst = pl.ds(cells - halo_cells, halo_cells), pl.ds(0, halo_cells)
        else:
            src, dst = pl.ds(0, halo_cells), pl.ds(halo_cells + cells, halo_cells)
        goal = lax.rem(c + k, clip_n)
        return pltpu.make_async_remote_copy(
            src_ref=packed.at[goal, :, src],
            dst_ref=landed.at[k, dt, :, dst],
            send_sem=frame_send.at[k, dt, dr + 1],
            recv_sem=frame_recv.at[k, dt, dr + 1],
            device_id={"clip": goal, "row": r + dr, "tm": t + dt},
            device_id_type=MESH,
        )

    moves = [
        (k, dt, dr)
        for k in range(clip_n - 1, -1, -1)
        for dt in (1, 0)
        for dr in (1, -1, 0)
        if (k, dt, dr) != (0, 0, 0)
    ]

    def each_move(sign, act):
        for k, dt, dr in moves:
            rr, tt = r + sign * dr, t + sign * dt
            if dr == 0 and dt == 0:
                act(frame_copy(k, dt, dr))
                continue

            @pl.when((rr >= 0) & (rr < row_dev) & (tt >= 0) & (tt < time_dev))
            def _():
                act(frame_copy(k, dt, dr))

    each_move(1, lambda copy: copy.start())
    landed[0, 0, :, halo_cells : halo_cells + cells] = packed[c]

    frames_wide = 2 * frame_n
    lines = frames_wide * chan
    depth = 256
    loads[3].wait()
    stem_w = stem_w_ref[...]
    taps_n = stem_w.shape[0]
    at = iota((depth, taps_n), 0)
    shift_at = quot(at, lines)
    in_shift = rest(at, lines)
    frame_at = quot(in_shift, chan)
    chan_at = in_shift - frame_at * chan
    tap_at = iota((depth, taps_n), 1)
    columns = []
    for f in range(ext_f):
        a = frame_at - f
        index = (a * (TAPS * TAPS) + shift_at) * chan + chan_at
        ok = (a >= 0) & (a < TAPS) & (at < TAPS * TAPS * lines) & (index == tap_at)
        columns.append(dot(one_hot(ok), stem_w).astype(BF16))
    stem_big = jnp.concatenate(columns, axis=1)

    lane = iota((128, 128), 1)
    source = iota((128, 128), 0)
    in_row = lane & (COLS - 1)
    col = 2 * (in_row & (COLS // 2 - 1)) + jnp.where(in_row >= COLS // 2, 1, 0)
    tables = []
    for tap in range(TAPS):
        moved = col + (tap - 1)
        ok = (moved >= 0) & (moved < COLS) & (source == (lane - in_row) + moved)
        tables.append(one_hot(ok))
    col_table = jnp.concatenate(tables, axis=1)

    half_rows = clips * per_clip
    total_rows = 2 * half_rows
    row_at = iota((total_rows, total_rows), 0)
    clip_at = quot(row_at, lines)
    in_clip = rest(row_at, lines)
    frame_at = quot(in_clip, chan)
    chan_at = in_clip - frame_at * chan
    base = clip_at * per_clip + chan_at
    before = jnp.where(t > 0, half_rows + base + frame_at * chan, base)
    goal = jnp.where(frame_at >= frame_n, base + (frame_at - frame_n) * chan, before)
    order = one_hot(goal == iota((total_rows, total_rows), 1))

    def group_table(chan_n):
        per_group = chan_n // GROUPS
        group_at = quot(iota((chan_n, chan_n), 0), per_group)
        return one_hot(group_at == quot(iota((chan_n, chan_n), 1), per_group))

    joined_mid, joined_out = group_table(chan_mid), group_table(chan_out)

    each_move(-1, lambda copy: copy.wait_recv())

    volume = landed[0].astype(F32)
    for k in range(1, clip_n):
        volume = volume + landed[k].astype(F32)
    volume = volume.astype(BF16).reshape(total_rows, wide)
    volume = dot(order, volume).astype(BF16)
    blocks = wide // 128
    stacked = jnp.concatenate(
        [volume[:, b * 128 : (b + 1) * 128] for b in range(blocks)], axis=0
    )
    shifted = dot(stacked, col_table)
    views = []
    by_tap = []
    for tap in range(TAPS):
        by_tap.append(
            jnp.concatenate(
                [
                    shifted[b * total_rows : (b + 1) * total_rows, tap * 128 : (tap + 1) * 128]
                    for b in range(blocks)
                ],
                axis=1,
            )
        )
    for row_tap in range(TAPS):
        for tap in range(TAPS):
            if row_tap % 2:
                views.append(
                    pltpu.roll(by_tap[tap], wide - row_tap * COLS, 1)[:, :out_cells]
                )
            else:
                views.append(by_tap[tap][:, row_tap * COLS : row_tap * COLS + out_cells])
    filler = jnp.zeros((depth - TAPS * TAPS * lines, out_cells), F32)

    def sum_copy(number, j):
        return pltpu.make_async_remote_copy(
            src_ref=sums[number].at[0],
            dst_ref=sums[number].at[j],
            send_sem=sum_send.at[number],
            recv_sem=sum_recv.at[number],
            device_id={"row": rows_at[j // time_dev], "tm": times_at[j % time_dev]},
            device_id_type=MESH,
        )

    def sum_wait(number, semaphore):
        others = sums[number].at[pl.ds(1, peers - 1)]
        pltpu.make_async_copy(others, others, semaphore.at[number]).wait()

    def send_sums(number, clip_sums):
        for place, (value_sum, square_sum) in enumerate(clip_sums):
            low = len(clip_sums) + place
            sums[number][0, place : place + 1, :] = value_sum
            sums[number][0, low : low + 1, :] = square_sum
        for j in range(1, peers):
            sum_copy(number, j).start()

    def take_sums(number, joined, gain, shift):
        sum_wait(number, sum_recv)
        total = sums[number][0]
        for j in range(1, peers):
            total = total + sums[number][j]
        rows = total.shape[0]
        high = total.astype(BF16).astype(F32)
        middle = (total - high).astype(BF16).astype(F32)
        low = total - high - middle
        joint = dot(jnp.concatenate([high, middle, low], axis=0).astype(BF16), joined)
        total = joint[:rows] + joint[rows : 2 * rows] + joint[2 * rows :]
        per_group = total.shape[1] // GROUPS
        total = total * (1.0 / (peers * frame_n * cells * per_group))
        mean = total[: rows // 2]
        inverse = lax.rsqrt(total[rows // 2 :] - mean * mean + eps)
        scale = inverse * gain
        move = shift - mean * scale
        return [(scale[i : i + 1], move[i : i + 1]) for i in range(rows // 2)]

    for number, group in enumerate(rounds1):
        clip_sums = []
        for k in group:
            patches = jnp.concatenate(
                [view[k * lines : (k + 1) * lines] for view in views] + [filler], axis=0
            ).astype(BF16)
            stem = lax.dot_general(
                patches, stem_big, (((0,), (0,)), ((), ())), preferred_element_type=F32
            )
            stem_scr[k] = stem
            own = stem[COLS : COLS + cells, HALO * chan_mid :]
            values = jnp.sum(own, axis=0, keepdims=True)
            squares = jnp.sum(own * own, axis=0, keepdims=True)
            value_sum = values[:, :chan_mid]
            square_sum = squares[:, :chan_mid]
            for f in range(1, frame_n):
                value_sum = value_sum + values[:, f * chan_mid : (f + 1) * chan_mid]
                square_sum = square_sum + squares[:, f * chan_mid : (f + 1) * chan_mid]
            clip_sums.append((value_sum, square_sum))
        send_sums(number, clip_sums)

    top = jnp.where(r > 0, 1.0, 0.0).astype(F32)
    bottom = jnp.where(r < row_dev - 1, 1.0, 0.0).astype(F32)
    ext_rows = row_n + 2
    half_cols = COLS // 2
    x_at = iota((ext_rows * half_cols, chan_mid), 0) & (half_cols - 1)

    def norm_first(k, frames_at, scale, shift):
        for f in frames_at:
            value = stem_scr[k, :, f * chan_mid : (f + 1) * chan_mid]
            value = silu(value * scale + shift)
            value = jnp.concatenate(
                [
                    value[:COLS] * top,
                    value[COLS : COLS + cells],
                    value[COLS + cells :] * bottom,
                ],
                axis=0,
            )
            parts = value.reshape(ext_rows, 2, half_cols, chan_mid)
            even, odd = parts[:, 0], parts[:, 1]
            flat = (ext_rows * half_cols, chan_mid)
            left = jnp.where(x_at == 0, 0.0, pltpu.roll(odd.reshape(flat), 1, 0))
            right = jnp.where(
                x_at == half_cols - 1, 0.0, pltpu.roll(even.reshape(flat), flat[0] - 1, 0)
            )
            left = left.reshape(even.shape)
            right = right.reshape(even.shape)
            before = jnp.stack([left, even], axis=1).reshape(value.shape)
            after = jnp.stack([odd, right], axis=1).reshape(value.shape)
            hidden_scr[k, f, :, :chan_mid] = before.astype(BF16)
            hidden_scr[k, f, :, chan_mid : 2 * chan_mid] = value.astype(BF16)
            hidden_scr[k, f, :, 2 * chan_mid :] = after.astype(BF16)

    def mix(k, first, count):
        strip = jnp.concatenate(
            [
                hidden_scr[k, first + a : first + a + count, b * COLS : b * COLS + cells, :].reshape(
                    count * cells, TAPS * chan_mid
                )
                for a in range(TAPS)
                for b in range(TAPS)
            ],
            axis=1,
        )
        mixed = dot(strip, mixer_w[...])
        mixer_scr[k, first : first + count] = mixed.reshape(count, cells, chan_out)
        return (
            jnp.sum(mixed, axis=0, keepdims=True),
            jnp.sum(mixed * mixed, axis=0, keepdims=True),
        )

    for load in loads[4:7]:
        load.wait()
    norms = {}

    def take_first(number):
        taken = take_sums(number, joined_mid, stem_gain_ref[...], stem_shift_ref[...])
        norms.update(zip(rounds1[number], taken))

    take_first(0)
    half = frame_n // 2
    norm_first(0, range(half + HALO), *norms[0])
    done = []
    for k in range(clips):
        low_sums = mix(k, 0, half)
        if k == 0:
            norm_first(0, range(half + HALO, ext_f), *norms[0])
        if k + 1 < clips:
            if k + 1 not in norms:
                take_first(1)
            norm_first(k + 1, range(ext_f), *norms[k + 1])
        high_sums = mix(k, half, frame_n - half)
        done.append((low_sums[0] + high_sums[0], low_sums[1] + high_sums[1]))
        for number, group in enumerate(rounds2):
            if group[-1] == k:
                send_sums(len(rounds1) + number, [done[i] for i in group])

    for load in loads[7:]:
        load.wait()
    bias = down_bias_ref[...]
    pairs = frame_n // 2
    out_rows = row_n // 2
    for number, group in enumerate(rounds2):
        taken = take_sums(
            len(rounds1) + number, joined_out, mixer_gain_ref[...], mixer_shift_ref[...]
        )
        for k, (scale, shift) in zip(group, taken):
            squares = []
            for pair in range(pairs):
                acts = []
                for f in (2 * pair, 2 * pair + 1):
                    value = mixer_scr[k, f] * scale + shift
                    acts.append(silu(value).astype(BF16).astype(F32))
                pooled = ((acts[0] + acts[1]) * 0.5).astype(BF16)
                pooled = pooled.reshape(out_rows, 2, 2, half_cols, chan_out)
                squares.append(
                    jnp.concatenate(
                        [
                            pooled[:, p, q].reshape(out_rows * half_cols, chan_out)
                            for p in range(2)
                            for q in range(2)
                        ],
                        axis=1,
                    )
                )
            block = jnp.concatenate(squares, axis=0)
            latent = dot(block, down_w[...]) + bias
            size = block.shape[0]
            out_ref[k * size : (k + 1) * size, :] = latent.astype(BF16)

    each_move(1, lambda copy: copy.wait_send())
    for number in range(len(sums)):
        sum_wait(number, sum_send)


def local(
    frames,
    keep_list,
    train_slot,
    stem_weight,
    stem_gain,
    stem_shift,
    mixer_weight,
    mixer_gain,
    mixer_shift,
    down_weight,
    down_bias,
):
    clip_n = lax.axis_size("clip")
    row_dev = lax.axis_size("row")
    time_dev = lax.axis_size("tm")
    slots, chan, frame_n, cells = frames.shape
    clips = train_slot.shape[0] // clip_n
    row_n = cells // COLS
    chan_mid = stem_weight.shape[1]
    chan_out = mixer_weight.shape[3]
    every = tuple(range(clips))
    rounds1 = tuple(part for part in (every[:1], every[1:]) if part)
    rounds2 = tuple(part for part in (every[:-1], every[-1:]) if part)
    peers = row_dev * time_dev
    ext_f = frame_n + HALO
    out_cells = cells + 2 * COLS
    sizes = (clip_n, row_dev, time_dev, clips, chan, frame_n, row_n, rounds1, rounds2)
    out_rows = clips * (frame_n // 2) * (row_n // 2) * (COLS // 2)
    operands = (
        frames,
        keep_list[None],
        train_slot[None],
        stem_weight,
        stem_gain[None],
        stem_shift[None],
        mixer_weight.reshape(-1, chan_out),
        mixer_gain[None],
        mixer_shift[None],
        down_weight,
        down_bias[None],
    )
    vmem = pl.BlockSpec(memory_space=pltpu.VMEM)
    hbm = pl.BlockSpec(memory_space=pltpu.HBM)
    out = pl.pallas_call(
        functools.partial(kernel, sizes),
        out_shape=jax.ShapeDtypeStruct((out_rows, chan_out), BF16),
        in_specs=[hbm] * len(operands),
        out_specs=vmem,
        scratch_shapes=[pltpu.VMEM(operand.shape, operand.dtype) for operand in operands]
        + [
            pltpu.VMEM((clip_n, clips * frame_n * chan, cells), BF16),
            pltpu.VMEM((clip_n, 2, clips * frame_n * chan, cells + 2 * HALO * COLS), BF16),
            pltpu.VMEM((clips, out_cells, ext_f * chan_mid), F32),
            pltpu.VMEM((clips, ext_f, out_cells, TAPS * chan_mid), BF16),
            pltpu.VMEM((clips, frame_n, cells, chan_out), F32),
            pltpu.SemaphoreType.DMA((len(operands),)),
            pltpu.SemaphoreType.DMA((clip_n, 2, 3)),
            pltpu.SemaphoreType.DMA((clip_n, 2, 3)),
            pltpu.SemaphoreType.DMA((len(rounds1) + len(rounds2),)),
            pltpu.SemaphoreType.DMA((len(rounds1) + len(rounds2),)),
        ]
        + [pltpu.VMEM((peers, 2 * len(part), chan_mid), F32) for part in rounds1]
        + [pltpu.VMEM((peers, 2 * len(part), chan_out), F32) for part in rounds2],
        compiler_params=pltpu.CompilerParams(
            collective_id=0, has_side_effects=True, vmem_limit_bytes=50 * 1024 * 1024
        ),
    )(*(pltpu.with_memory_space_constraint(operand, pltpu.HBM) for operand in operands))
    return out.reshape(clips, frame_n // 2, row_n // 2, COLS // 2, chan_out)


def solution(mesh):
    return jax.shard_map(
        local,
        mesh=mesh,
        in_specs=(
            P("clip", None, "tm", "row"),
            P("clip"),
            P(),
            P(),
            P(),
            P(),
            P(),
            P(),
            P(),
            P(),
            P(),
        ),
        out_specs=P("clip", "tm", "row", None, None),
        check_vma=False,
    )
```

```python
import functools

import jax
import jax.numpy as jnp
from jax import lax
from jax.experimental import pallas as pl
from jax.experimental.pallas import tpu as pltpu
from jax.sharding import PartitionSpec as P

GROUPS = 32
COLS = 64
HALO = 2
TAPS = 3
MESH = pl.DeviceIdType.MESH
F32 = jnp.float32
BF16 = jnp.bfloat16

eps = 1e-06


def iota(shape, dim):
    return lax.broadcasted_iota(jnp.int32, shape, dim)


def quot(value, by):
    return lax.shift_right_logical(value * (65536 // by + 1), 16)


def rest(value, by):
    return value - quot(value, by) * by


def dot(left, right):
    return jnp.dot(left, right, preferred_element_type=F32)


def silu(value):
    half = value * 0.5
    return half + half * jnp.tanh(half)


def one_hot(flag):
    return jnp.where(flag, 1.0, 0.0).astype(BF16)


def kernel(
    sizes,
    frames_hbm,
    keep_hbm,
    train_hbm,
    stem_w_hbm,
    stem_gain_hbm,
    stem_shift_hbm,
    mixer_w_hbm,
    mixer_gain_hbm,
    mixer_shift_hbm,
    down_w_hbm,
    down_bias_hbm,
    out_ref,
    frames_ref,
    keep_ref,
    train_ref,
    stem_w_ref,
    stem_gain_ref,
    stem_shift_ref,
    mixer_w,
    mixer_gain_ref,
    mixer_shift_ref,
    down_w,
    down_bias_ref,
    packed,
    landed,
    stem_scr,
    hidden_scr,
    mixer_scr,
    load_sem,
    frame_send,
    frame_recv,
    sum_send,
    sum_recv,
    *sums,
):
    clip_n, row_dev, time_dev, clips, chan, frame_n, row_n, rounds1, rounds2 = sizes
    cells = row_n * COLS
    c = lax.axis_index("clip")
    r = lax.axis_index("row")
    t = lax.axis_index("tm")
    rows_at = [jnp.where(r + j < row_dev, r + j, r + j - row_dev) for j in range(row_dev)]
    times_at = [jnp.where(t + j < time_dev, t + j, t + j - time_dev) for j in range(time_dev)]
    peers = row_dev * time_dev
    per_clip = frame_n * chan
    halo_cells = HALO * COLS
    wide = cells + 2 * halo_cells
    out_cells = cells + 2 * COLS
    ext_f = frame_n + HALO
    chan_mid = stem_w_ref.shape[1]
    chan_out = mixer_w.shape[1]

    loads = [
        pltpu.make_async_copy(source, target, load_sem.at[number])
        for number, (source, target) in enumerate(
            (
                (frames_hbm, frames_ref),
                (keep_hbm, keep_ref),
                (train_hbm, train_ref),
                (stem_w_hbm, stem_w_ref),
                (stem_gain_hbm, stem_gain_ref),
                (stem_shift_hbm, stem_shift_ref),
                (mixer_w_hbm, mixer_w),
                (mixer_gain_hbm, mixer_gain_ref),
                (mixer_shift_hbm, mixer_shift_ref),
                (down_w_hbm, down_w),
                (down_bias_hbm, down_bias_ref),
            )
        )
    ]
    for load in loads:
        load.start()

    landed[...] = jnp.zeros_like(landed)

    barrier = pltpu.get_barrier_semaphore()
    for j in range(1, peers):
        pl.semaphore_signal(
            barrier,
            inc=1,
            device_id={"row": rows_at[j // time_dev], "tm": times_at[j % time_dev]},
            device_id_type=MESH,
        )
    rows_near = 1 + (r > 0).astype(jnp.int32) + (r < row_dev - 1).astype(jnp.int32)
    times_near = 1 + (t > 0).astype(jnp.int32) + (t < time_dev - 1).astype(jnp.int32)
    for k in range(1, clip_n):
        for dr in (-1, 0, 1):
            for dt in (-1, 0, 1):

                @pl.when((r + dr >= 0) & (r + dr < row_dev) & (t + dt >= 0) & (t + dt < time_dev))
                def _():
                    pl.semaphore_signal(
                        barrier,
                        inc=1,
                        device_id={"clip": lax.rem(c + k, clip_n), "row": r + dr, "tm": t + dt},
                        device_id_type=MESH,
                    )

    for load in loads[:3]:
        load.wait()

    slot_n = keep_ref.shape[1]
    enc_n = train_ref.shape[1]
    rows_in = slot_n * per_clip
    rows_out = enc_n * per_clip
    named = one_hot(iota((enc_n, slot_n), 0) == keep_ref[...])
    spread = one_hot(quot(iota((slot_n, rows_in), 1), per_clip) == iota((slot_n, rows_in), 0))
    by_row = dot(named, spread).astype(BF16)
    wanted = one_hot(quot(iota((rows_out, enc_n), 0), per_clip) == train_ref[...])
    chosen = dot(wanted, by_row)
    row_at = rest(iota((rows_out, rows_in), 0), per_clip)
    col_at = rest(iota((rows_out, rows_in), 1), per_clip)
    same = (quot(row_at, chan) == rest(col_at, frame_n)) & (
        rest(row_at, chan) == quot(col_at, frame_n)
    )
    chosen = jnp.where(same, chosen, 0.0).astype(BF16)
    flat_frames = jnp.concatenate(
        [frames_ref[s, i].astype(F32) for s in range(slot_n) for i in range(chan)], axis=0
    ).astype(BF16)
    picked = dot(chosen, flat_frames).astype(BF16)
    packed[...] = picked.reshape(packed.shape)

    pl.semaphore_wait(barrier, peers - 1 + (clip_n - 1) * rows_near * times_near)

    def frame_copy(k, dt, dr):
        if dr == 0:
            src, dst = pl.ds(0, cells), pl.ds(halo_cells, cells)
        elif dr == 1:
            src, dst = pl.ds(cells - halo_cells, halo_cells), pl.ds(0, halo_cells)
        else:
            src, dst = pl.ds(0, halo_cells), pl.ds(halo_cells + cells, halo_cells)
        goal = lax.rem(c + k, clip_n)
        return pltpu.make_async_remote_copy(
            src_ref=packed.at[goal, :, src],
            dst_ref=landed.at[k, dt, :, dst],
            send_sem=frame_send.at[k, dt, dr + 1],
            recv_sem=frame_recv.at[k, dt, dr + 1],
            device_id={"clip": goal, "row": r + dr, "tm": t + dt},
            device_id_type=MESH,
        )

    moves = [
        (k, dt, dr)
        for k in range(clip_n - 1, -1, -1)
        for dt in (1, 0)
        for dr in (1, -1, 0)
        if (k, dt, dr) != (0, 0, 0)
    ]

    def each_move(sign, act):
        for k, dt, dr in moves:
            rr, tt = r + sign * dr, t + sign * dt
            if dr == 0 and dt == 0:
                act(frame_copy(k, dt, dr))
                continue

            @pl.when((rr >= 0) & (rr < row_dev) & (tt >= 0) & (tt < time_dev))
            def _():
                act(frame_copy(k, dt, dr))

    each_move(1, lambda copy: copy.start())
    landed[0, 0, :, halo_cells : halo_cells + cells] = packed[c]

    frames_wide = 2 * frame_n
    lines = frames_wide * chan
    depth = 256
    loads[3].wait()
    stem_w = stem_w_ref[...]
    taps_n = stem_w.shape[0]
    at = iota((depth, taps_n), 0)
    shift_at = quot(at, lines)
    in_shift = rest(at, lines)
    frame_at = quot(in_shift, chan)
    chan_at = in_shift - frame_at * chan
    tap_at = iota((depth, taps_n), 1)
    columns = []
    for f in range(ext_f):
        a = frame_at - f
        index = (a * (TAPS * TAPS) + shift_at) * chan + chan_at
        ok = (a >= 0) & (a < TAPS) & (at < TAPS * TAPS * lines) & (index == tap_at)
        columns.append(dot(one_hot(ok), stem_w).astype(BF16))
    stem_big = jnp.concatenate(columns, axis=1)

    lane = iota((128, 128), 1)
    source = iota((128, 128), 0)
    in_row = lane & (COLS - 1)
    col = 2 * (in_row & (COLS // 2 - 1)) + jnp.where(in_row >= COLS // 2, 1, 0)
    tables = []
    for tap in range(TAPS):
        moved = col + (tap - 1)
        ok = (moved >= 0) & (moved < COLS) & (source == (lane - in_row) + moved)
        tables.append(one_hot(ok))
    col_table = jnp.concatenate(tables, axis=1)

    half_rows = clips * per_clip
    total_rows = 2 * half_rows
    row_at = iota((total_rows, total_rows), 0)
    clip_at = quot(row_at, lines)
    in_clip = rest(row_at, lines)
    frame_at = quot(in_clip, chan)
    chan_at = in_clip - frame_at * chan
    base = clip_at * per_clip + chan_at
    before = jnp.where(t > 0, half_rows + base + frame_at * chan, base)
    goal = jnp.where(frame_at >= frame_n, base + (frame_at - frame_n) * chan, before)
    order = one_hot(goal == iota((total_rows, total_rows), 1))

    def group_table(chan_n):
        per_group = chan_n // GROUPS
        group_at = quot(iota((chan_n, chan_n), 0), per_group)
        return one_hot(group_at == quot(iota((chan_n, chan_n), 1), per_group))

    joined_mid, joined_out = group_table(chan_mid), group_table(chan_out)

    each_move(-1, lambda copy: copy.wait_recv())

    volume = landed[0].astype(F32)
    for k in range(1, clip_n):
        volume = volume + landed[k].astype(F32)
    volume = volume.astype(BF16).reshape(total_rows, wide)
    volume = dot(order, volume).astype(BF16)
    blocks = wide // 128
    stacked = jnp.concatenate(
        [volume[:, b * 128 : (b + 1) * 128] for b in range(blocks)], axis=0
    )
    shifted = dot(stacked, col_table)
    views = []
    by_tap = []
    for tap in range(TAPS):
        by_tap.append(
            jnp.concatenate(
                [
                    shifted[b * total_rows : (b + 1) * total_rows, tap * 128 : (tap + 1) * 128]
                    for b in range(blocks)
                ],
                axis=1,
            )
        )
    for row_tap in range(TAPS):
        for tap in range(TAPS):
            if row_tap % 2:
                views.append(
                    pltpu.roll(by_tap[tap], wide - row_tap * COLS, 1)[:, :out_cells]
                )
            else:
                views.append(by_tap[tap][:, row_tap * COLS : row_tap * COLS + out_cells])
    filler = jnp.zeros((depth - TAPS * TAPS * lines, out_cells), F32)

    def sum_copy(number, j):
        return pltpu.make_async_remote_copy(
            src_ref=sums[number].at[0],
            dst_ref=sums[number].at[j],
            send_sem=sum_send.at[number],
            recv_sem=sum_recv.at[number],
            device_id={"row": rows_at[j // time_dev], "tm": times_at[j % time_dev]},
            device_id_type=MESH,
        )

    def sum_wait(number, semaphore):
        others = sums[number].at[pl.ds(1, peers - 1)]
        pltpu.make_async_copy(others, others, semaphore.at[number]).wait()

    def send_sums(number, clip_sums):
        for place, (value_sum, square_sum) in enumerate(clip_sums):
            low = len(clip_sums) + place
            sums[number][0, place : place + 1, :] = value_sum
            sums[number][0, low : low + 1, :] = square_sum
        for j in range(1, peers):
            sum_copy(number, j).start()

    def take_sums(number, joined, gain, shift):
        sum_wait(number, sum_recv)
        total = sums[number][0]
        for j in range(1, peers):
            total = total + sums[number][j]
        rows = total.shape[0]
        high = total.astype(BF16).astype(F32)
        middle = (total - high).astype(BF16).astype(F32)
        low = total - high - middle
        joint = dot(jnp.concatenate([high, middle, low], axis=0).astype(BF16), joined)
        total = joint[:rows] + joint[rows : 2 * rows] + joint[2 * rows :]
        per_group = total.shape[1] // GROUPS
        total = total * (1.0 / (peers * frame_n * cells * per_group))
        mean = total[: rows // 2]
        inverse = lax.rsqrt(total[rows // 2 :] - mean * mean + eps)
        scale = inverse * gain
        move = shift - mean * scale
        return [(scale[i : i + 1], move[i : i + 1]) for i in range(rows // 2)]

    for number, group in enumerate(rounds1):
        clip_sums = []
        for k in group:
            patches = jnp.concatenate(
                [view[k * lines : (k + 1) * lines] for view in views] + [filler], axis=0
            ).astype(BF16)
            stem = lax.dot_general(
                patches, stem_big, (((0,), (0,)), ((), ())), preferred_element_type=F32
            )
            stem_scr[k] = stem
            own = stem[COLS : COLS + cells, HALO * chan_mid :]
            values = jnp.sum(own, axis=0, keepdims=True)
            squares = jnp.sum(own * own, axis=0, keepdims=True)
            value_sum = values[:, :chan_mid]
            square_sum = squares[:, :chan_mid]
            for f in range(1, frame_n):
                value_sum = value_sum + values[:, f * chan_mid : (f + 1) * chan_mid]
                square_sum = square_sum + squares[:, f * chan_mid : (f + 1) * chan_mid]
            clip_sums.append((value_sum, square_sum))
        send_sums(number, clip_sums)

    top = jnp.where(r > 0, 1.0, 0.0).astype(F32)
    bottom = jnp.where(r < row_dev - 1, 1.0, 0.0).astype(F32)
    ext_rows = row_n + 2
    half_cols = COLS // 2
    x_at = iota((ext_rows * half_cols, chan_mid), 0) & (half_cols - 1)

    def norm_first(k, frames_at, scale, shift):
        for f in frames_at:
            value = stem_scr[k, :, f * chan_mid : (f + 1) * chan_mid]
            value = silu(value * scale + shift)
            value = jnp.concatenate(
                [
                    value[:COLS] * top,
                    value[COLS : COLS + cells],
                    value[COLS + cells :] * bottom,
                ],
                axis=0,
            )
            parts = value.reshape(ext_rows, 2, half_cols, chan_mid)
            even, odd = parts[:, 0], parts[:, 1]
            flat = (ext_rows * half_cols, chan_mid)
            left = jnp.where(x_at == 0, 0.0, pltpu.roll(odd.reshape(flat), 1, 0))
            right = jnp.where(
                x_at == half_cols - 1, 0.0, pltpu.roll(even.reshape(flat), flat[0] - 1, 0)
            )
            left = left.reshape(even.shape)
            right = right.reshape(even.shape)
            before = jnp.stack([left, even], axis=1).reshape(value.shape)
            after = jnp.stack([odd, right], axis=1).reshape(value.shape)
            hidden_scr[k, f, :, :chan_mid] = before.astype(BF16)
            hidden_scr[k, f, :, chan_mid : 2 * chan_mid] = value.astype(BF16)
            hidden_scr[k, f, :, 2 * chan_mid :] = after.astype(BF16)

    def mix(k, first, count):
        strip = jnp.concatenate(
            [
                hidden_scr[k, first + a : first + a + count, b * COLS : b * COLS + cells, :].reshape(
                    count * cells, TAPS * chan_mid
                )
                for a in range(TAPS)
                for b in range(TAPS)
            ],
            axis=1,
        )
        mixed = dot(strip, mixer_w[...])
        mixer_scr[k, first : first + count] = mixed.reshape(count, cells, chan_out)
        return (
            jnp.sum(mixed, axis=0, keepdims=True),
            jnp.sum(mixed * mixed, axis=0, keepdims=True),
        )

    for load in loads[4:7]:
        load.wait()
    norms = {}

    def take_first(number):
        taken = take_sums(number, joined_mid, stem_gain_ref[...], stem_shift_ref[...])
        norms.update(zip(rounds1[number], taken))

    take_first(0)
    done = []
    norm_first(0, range(TAPS), *norms[0])
    for k in range(clips):
        parts = []
        for f in range(frame_n):
            parts.append(mix(k, f, 1))
            if k == 0 and f + TAPS < ext_f:
                norm_first(0, (f + TAPS,), *norms[0])
            if k + 1 < clips and f > 0:
                if k + 1 not in norms:
                    take_first(1)
                low = (f - 1) * ext_f // (frame_n - 1)
                norm_first(k + 1, range(low, f * ext_f // (frame_n - 1)), *norms[k + 1])
        done.append((sum(part[0] for part in parts), sum(part[1] for part in parts)))
        for number, group in enumerate(rounds2):
            if group[-1] == k:
                send_sums(len(rounds1) + number, [done[i] for i in group])

    for load in loads[7:]:
        load.wait()
    bias = down_bias_ref[...]
    pairs = frame_n // 2
    out_rows = row_n // 2
    for number, group in enumerate(rounds2):
        taken = take_sums(
            len(rounds1) + number, joined_out, mixer_gain_ref[...], mixer_shift_ref[...]
        )
        for k, (scale, shift) in zip(group, taken):
            squares = []
            for pair in range(pairs):
                acts = []
                for f in (2 * pair, 2 * pair + 1):
                    value = mixer_scr[k, f] * scale + shift
                    acts.append(silu(value).astype(BF16).astype(F32))
                pooled = ((acts[0] + acts[1]) * 0.5).astype(BF16)
                pooled = pooled.reshape(out_rows, 2, 2, half_cols, chan_out)
                squares.append(
                    jnp.concatenate(
                        [
                            pooled[:, p, q].reshape(out_rows * half_cols, chan_out)
                            for p in range(2)
                            for q in range(2)
                        ],
                        axis=1,
                    )
                )
            block = jnp.concatenate(squares, axis=0)
            latent = dot(block, down_w[...]) + bias
            size = block.shape[0]
            out_ref[k * size : (k + 1) * size, :] = latent.astype(BF16)

    each_move(1, lambda copy: copy.wait_send())
    for number in range(len(sums)):
        sum_wait(number, sum_send)


def local(
    frames,
    keep_list,
    train_slot,
    stem_weight,
    stem_gain,
    stem_shift,
    mixer_weight,
    mixer_gain,
    mixer_shift,
    down_weight,
    down_bias,
):
    clip_n = lax.axis_size("clip")
    row_dev = lax.axis_size("row")
    time_dev = lax.axis_size("tm")
    slots, chan, frame_n, cells = frames.shape
    clips = train_slot.shape[0] // clip_n
    row_n = cells // COLS
    chan_mid = stem_weight.shape[1]
    chan_out = mixer_weight.shape[3]
    every = tuple(range(clips))
    rounds1 = tuple(part for part in (every[:1], every[1:]) if part)
    rounds2 = tuple(part for part in (every[:-1], every[-1:]) if part)
    peers = row_dev * time_dev
    ext_f = frame_n + HALO
    out_cells = cells + 2 * COLS
    sizes = (clip_n, row_dev, time_dev, clips, chan, frame_n, row_n, rounds1, rounds2)
    out_rows = clips * (frame_n // 2) * (row_n // 2) * (COLS // 2)
    operands = (
        frames,
        keep_list[None],
        train_slot[None],
        stem_weight,
        stem_gain[None],
        stem_shift[None],
        mixer_weight.reshape(-1, chan_out),
        mixer_gain[None],
        mixer_shift[None],
        down_weight,
        down_bias[None],
    )
    vmem = pl.BlockSpec(memory_space=pltpu.VMEM)
    hbm = pl.BlockSpec(memory_space=pltpu.HBM)
    out = pl.pallas_call(
        functools.partial(kernel, sizes),
        out_shape=jax.ShapeDtypeStruct((out_rows, chan_out), BF16),
        in_specs=[hbm] * len(operands),
        out_specs=vmem,
        scratch_shapes=[pltpu.VMEM(operand.shape, operand.dtype) for operand in operands]
        + [
            pltpu.VMEM((clip_n, clips * frame_n * chan, cells), BF16),
            pltpu.VMEM((clip_n, 2, clips * frame_n * chan, cells + 2 * HALO * COLS), BF16),
            pltpu.VMEM((clips, out_cells, ext_f * chan_mid), F32),
            pltpu.VMEM((clips, ext_f, out_cells, TAPS * chan_mid), BF16),
            pltpu.VMEM((clips, frame_n, cells, chan_out), F32),
            pltpu.SemaphoreType.DMA((len(operands),)),
            pltpu.SemaphoreType.DMA((clip_n, 2, 3)),
            pltpu.SemaphoreType.DMA((clip_n, 2, 3)),
            pltpu.SemaphoreType.DMA((len(rounds1) + len(rounds2),)),
            pltpu.SemaphoreType.DMA((len(rounds1) + len(rounds2),)),
        ]
        + [pltpu.VMEM((peers, 2 * len(part), chan_mid), F32) for part in rounds1]
        + [pltpu.VMEM((peers, 2 * len(part), chan_out), F32) for part in rounds2],
        compiler_params=pltpu.CompilerParams(
            collective_id=0, has_side_effects=True, vmem_limit_bytes=50 * 1024 * 1024
        ),
    )(*(pltpu.with_memory_space_constraint(operand, pltpu.HBM) for operand in operands))
    return out.reshape(clips, frame_n // 2, row_n // 2, COLS // 2, chan_out)


def solution(mesh):
    return jax.shard_map(
        local,
        mesh=mesh,
        in_specs=(
            P("clip", None, "tm", "row"),
            P("clip"),
            P(),
            P(),
            P(),
            P(),
            P(),
            P(),
            P(),
            P(),
            P(),
        ),
        out_specs=P("clip", "tm", "row", None, None),
        check_vma=False,
    )
```
